512 devices in a mesh: prompt: 32 (over y_hi, x, core), resp: 16 (over y_lo, z).
Axes of the slice: x: 4, y: 8 (y_hi: 4, y_lo: 2; y = y_hi * 2 + y_lo), z: 8, core: 2. Of those that a mesh axis runs over, the one named last changes fastest.
Arguments:
- prefix_keys: bfloat16 [32, 512, 512], P('prompt', 'resp'), may hold values from -6 to 6
- prefix_values: bfloat16 [32, 512, 512], P('prompt', 'resp'), may hold values from -6 to 6
- resp_queries: bfloat16 [32, 16, 128, 2560], P('prompt', 'resp'), may hold values from -6 to 6
- resp_keys: bfloat16 [32, 16, 128, 512], P('prompt', 'resp'), may hold values from -6 to 6
- resp_values: bfloat16 [32, 16, 128, 512], P('prompt', 'resp'), may hold values from -6 to 6
- query_bias: float32 [2560], replicated, may hold values from -3 to 3
- out_grad: bfloat16 [32, 16, 128, 2560], P('prompt', 'resp'), may hold values from -96 to 96
- lengths: int32 [32, 16], P('prompt', 'resp'), may hold values from 16 to 128, as said below
Outputs:
- grad_queries: bfloat16 [32, 16, 128, 2560], P('prompt', 'resp')
- grad_resp_keys: bfloat16 [32, 16, 128, 512], P('prompt', 'resp')
- grad_resp_values: bfloat16 [32, 16, 128, 512], P('prompt', 'resp')
- grad_prefix_keys: bfloat16 [32, 512, 512], P('prompt', 'resp')
- grad_prefix_values: bfloat16 [32, 512, 512], P('prompt', 'resp')
- grad_query_bias: float32 [2560], replicated
The draws below stay inside these ranges and needn't reach their ends.
Inputs may be any that keep to these rules, and one draw needn't show every extreme that they name: `lengths`: every prompt has one response of exactly 128 live tokens.
All inputs are finite; a program needn't handle non-finite values.
Results may differ from the reference program's by a relative error of at most 0.025.
Values may be sent and summed in bfloat16 or wider, within the bound.
No kernel may reach another device: no remote copies, remote signals or barrier semaphores. Data moves between devices by JAX's collectives and lax.ppermute only.
A program may use at most 64 MiB of HBM per device.

```python
import math
import jax
import jax.numpy as jnp
from jax import lax

HD = 128
KVH = 4
GROUP = 5
QH = 20
ROWS = 128
PRE = 512
PROMPTS = 32
RESP = 16
N_PROMPT = 32
N_RESP = 16


def draw_resp_queries(key, part):
    key = jax.random.fold_in(key, 5)
    shape = (PROMPTS, RESP, ROWS, QH * HD)
    values = jax.random.truncated_normal(key, -5.5, 5.5, shape, jnp.float32)
    return values.astype(jnp.bfloat16)


def draw_prefix_keys(key, part):
    key = jax.random.fold_in(key, 7)
    shape = (PROMPTS, PRE, KVH * HD)
    values = jax.random.truncated_normal(key, -5.5, 5.5, shape, jnp.float32)
    return values.astype(jnp.bfloat16)


def draw_lengths(key, part):
    key = jax.random.fold_in(key, 9)
    first_key, second_key = jax.random.split(key)
    drawn = jax.random.randint(first_key, (PROMPTS, RESP), ROWS // 8, ROWS + 1)
    chosen = jax.random.randint(second_key, (PROMPTS, 1), 0, RESP)
    slots = lax.broadcasted_iota(jnp.int32, (PROMPTS, RESP), 1)
    return jnp.where(slots == chosen, ROWS, drawn).astype(jnp.int32)


def block_levels(rng, extent, cuts, smallest, high):
    level = 1.0
    for axis_at, shards_of in cuts:
        draws = jax.random.uniform(jax.random.fold_in(jax.random.fold_in(rng, 6), axis_at), (shards_of,), jnp.float32, smallest / len(cuts), high / len(cuts))
        level = level * jnp.repeat(jnp.exp(draws), extent[axis_at] // shards_of).reshape((-1,) + (1,) * (len(extent) - 1 - axis_at))
    return level


def bell_draw(key, extent, scale, bound, cuts=(), kind=jnp.bfloat16):
    factor_of = block_levels(key, extent, cuts, -0.22, 0.18) if cuts else 1.0
    values = jax.random.normal(key, extent, jnp.float32) * scale * factor_of
    return jnp.minimum(jnp.maximum(values, -bound), bound).astype(kind)


def setup_inputs(seed: int = 0) -> dict:
    key_of = jax.random.split(jax.random.key(seed), 9)
    return {
        "prefix_keys": draw_prefix_keys(jax.random.fold_in(key_of[8], 71), 0),
        "prefix_values": bell_draw(key_of[1], (PROMPTS, PRE, KVH * HD), 1.0, 6.0, ((0, 32), (1, 16))),
        "resp_queries": draw_resp_queries(jax.random.fold_in(key_of[8], 71), 0),
        "resp_keys": bell_draw(key_of[3], (PROMPTS, RESP, ROWS, KVH * HD), 1.0, 6.0, ((0, 32), (1, 16))),
        "resp_values": bell_draw(key_of[4], (PROMPTS, RESP, ROWS, KVH * HD), 1.0, 6.0, ((0, 32), (1, 16))),
        "query_bias": bell_draw(key_of[5], (QH * HD,), 0.5, 3.0, (), jnp.float32),
        "out_grad": bell_draw(key_of[6], (PROMPTS, RESP, ROWS, QH * HD), 16.0, 96.0, ((0, 32), (1, 16))),
        "lengths": draw_lengths(jax.random.fold_in(key_of[8], 71), 0),
    }


def response_grads(queries, resp_k, resp_v, pre_k, pre_v, dout, length):
    f32 = jnp.float32
    row_count = queries.shape[0]
    prefix_count = pre_k.shape[0]
    key_count = prefix_count + row_count
    keys = jnp.concatenate([pre_k, resp_k], 0).astype(f32).reshape(key_count, KVH, HD)
    values = jnp.concatenate([pre_v, resp_v], 0).astype(f32).reshape(key_count, KVH, HD)
    rows = lax.broadcasted_iota(jnp.int32, (row_count, key_count), 0)
    cols = lax.broadcasted_iota(jnp.int32, (row_count, key_count), 1)
    later = cols - prefix_count
    visible = (cols < prefix_count) | (later <= rows) & (later < length)
    live = rows[:, :1] < length
    dout = jnp.where(live, dout, jnp.zeros((), jnp.bfloat16))
    q_four = queries.astype(f32).reshape(row_count, KVH, GROUP, HD)
    do_four = dout.astype(f32).reshape(row_count, KVH, GROUP, HD)
    scale = 1.0 / math.sqrt(HD)
    scores = jnp.einsum('igch,jgh->gcij', q_four, keys) * scale
    scores = jnp.where(visible, scores, -jnp.inf)
    top = lax.optimization_barrier(jnp.max(scores, -1, keepdims=True))
    expd = jnp.exp(scores - top)
    total = lax.optimization_barrier(jnp.sum(expd, -1, keepdims=True))
    probs = expd / total
    probs_low = lax.optimization_barrier(probs.astype(jnp.bfloat16)).astype(f32)
    dprobs = jnp.einsum('igch,jgh->gcij', do_four, values)
    delta = lax.optimization_barrier(jnp.sum(probs * dprobs, -1, keepdims=True))
    dscores = lax.optimization_barrier((probs * (dprobs - delta) * scale).astype(jnp.bfloat16)).astype(f32)
    grad_q = jnp.einsum('gcij,jgh->igch', dscores, keys).reshape(row_count, QH * HD)
    grad_k = jnp.einsum('gcij,igch->jgh', dscores, q_four).reshape(key_count, KVH * HD)
    grad_v = jnp.einsum('gcij,igch->jgh', probs_low, do_four).reshape(key_count, KVH * HD)
    return (grad_q, grad_k, grad_v)

def reference(prefix_keys, prefix_values, resp_queries, resp_keys, resp_values, query_bias, out_grad, lengths):
    queries = (resp_queries.astype(jnp.float32) + query_bias.astype(jnp.float32)).astype(jnp.bfloat16)

    def per_prompt(items):
        pre_k, pre_v, q_all, k_all, v_all, do_all, len_all = items

        def per_resp(inner):
            return response_grads(inner[0], inner[1], inner[2], pre_k, pre_v, inner[3], inner[4])
        grad_q, grad_k, grad_v = lax.map(per_resp, (q_all, k_all, v_all, do_all, len_all))
        prefix_count = pre_k.shape[0]
        pre_dk = lax.optimization_barrier(jnp.sum(grad_k[:, :prefix_count], 0)).astype(jnp.bfloat16)
        pre_dv = lax.optimization_barrier(jnp.sum(grad_v[:, :prefix_count], 0)).astype(jnp.bfloat16)
        bias_part = lax.optimization_barrier(jnp.sum(grad_q, axis=(0, 1)))
        return (grad_q.astype(jnp.bfloat16), grad_k[:, prefix_count:].astype(jnp.bfloat16), grad_v[:, prefix_count:].astype(jnp.bfloat16), pre_dk, pre_dv, bias_part)
    results = lax.map(per_prompt, (prefix_keys, prefix_values, queries, resp_keys, resp_values, out_grad, lengths))
    grad_bias = lax.optimization_barrier(jnp.sum(results[5], 0)) / math.sqrt(N_PROMPT * N_RESP * ROWS)
    return (results[0], results[1], results[2], results[3], results[4], grad_bias)
```

```python
import functools
import math

import jax
import jax.numpy as jnp
from jax import lax
from jax.experimental import pallas as pl
from jax.experimental.pallas import tpu as pltpu
from jax.sharding import PartitionSpec as P

HD = 128
GROUP = 5
KVH = 4
SCALE = 1.0 / math.sqrt(HD)
LOG2E = 1.4426950408889634
F32 = jnp.float32
BF16 = jnp.bfloat16


def dot(a, b, a_dim, b_dim):
    return lax.dot_general(a, b, (((a_dim,), (b_dim,)), ((), ())), preferred_element_type=F32)


def attend_kernel(
    length_ref, q_ref, bias_ref, do_ref, rk_ref, rv_ref, kv_ref,
    dq_ref, drk_ref, drv_ref, pre_ref, bias_sum, probs_s, dscores_s, q_s, do_s,
):
    group = pl.program_id(0)
    length = length_ref[0, 0]
    rows = q_ref.shape[0]
    shards, _, shard_rows, _ = kv_ref.shape
    prefix = shards * shard_rows
    keys = jnp.concatenate([kv_ref[:, 0].reshape(prefix, HD), rk_ref[...]], 0)
    values = jnp.concatenate([kv_ref[:, 1].reshape(prefix, HD), rv_ref[...]], 0)
    live = lax.broadcasted_iota(jnp.int32, (rows, HD), 0) < length
    key_at = lax.broadcasted_iota(jnp.int32, (rows, rows), 0)
    row_at = lax.broadcasted_iota(jnp.int32, (rows, rows), 1)
    visible = (key_at <= row_at) & (key_at < length)
    for head in range(GROUP):
        cols = slice(head * HD, (head + 1) * HD)
        span = slice(head * rows, (head + 1) * rows)
        q = (q_ref[:, cols].astype(F32) + bias_ref[:, cols]).astype(BF16)
        do = jnp.where(live, do_ref[:, cols].astype(F32), 0.0).astype(BF16)
        q_s[span, :] = q
        do_s[span, :] = do
        scores = dot(keys, q, 1, 1) * (SCALE * LOG2E)
        scores = jnp.concatenate(
            [scores[:prefix], jnp.where(visible, scores[prefix:], -jnp.inf)], 0
        )
        expd = jnp.exp2(scores - jnp.max(scores, 0, keepdims=True))
        inverse = 1.0 / jnp.sum(expd, 0, keepdims=True)
        probs = expd * inverse
        dprobs = dot(values, do, 1, 1)
        delta = jnp.sum(probs * dprobs, 0, keepdims=True)
        probs_s[:, span] = probs.astype(BF16)
        dscores_s[:, span] = (probs * (dprobs - delta) * SCALE).astype(BF16)
    dscores = dscores_s[...]
    dk = dot(dscores, q_s[...], 1, 0)
    dv = dot(probs_s[...], do_s[...], 1, 0)
    pre_ref[:, 2 * group] = dk[:prefix].astype(BF16).reshape(shards, shard_rows, HD)
    pre_ref[:, 2 * group + 1] = dv[:prefix].astype(BF16).reshape(shards, shard_rows, HD)
    drk_ref[...] = dk[prefix:].astype(BF16)
    drv_ref[...] = dv[prefix:].astype(BF16)
    dq_t = dot(keys, dscores, 0, 0)
    for head in range(GROUP):
        dq = dq_t[:, head * rows : (head + 1) * rows].T
        dq_ref[:, head * HD : (head + 1) * HD] = dq.astype(BF16)
        bias_sum[pl.ds(group * GROUP + head, 1), :] = jnp.sum(dq, 0, keepdims=True)

    @pl.when(group == pl.num_programs(0) - 1)
    def _():
        per = 2
        heads = KVH * GROUP
        total = bias_sum[...]
        high = total.astype(BF16).astype(F32)
        middle = (total - high).astype(BF16).astype(F32)
        low = total - high - middle
        for shard in range(shards):
            if shard * per < heads:
                at = slice(shard * per, (shard + 1) * per)
                block = jnp.concatenate(
                    [high[at], middle[at], low[at], jnp.zeros((shard_rows - 3 * per, HD), F32)], 0
                )
            else:
                block = jnp.zeros((shard_rows, HD), F32)
            pre_ref[shard, 2 * KVH] = block.astype(BF16)


def attend(length, queries, bias, cotangent, resp_keys, resp_values, gathered):
    rows, width = queries.shape
    shards, _, shard_rows, _ = gathered.shape
    key_count = shards * shard_rows + rows
    wide = GROUP * HD
    heads_out = 2 * KVH + 1
    column = lambda g: (0, g)
    return pl.pallas_call(
        attend_kernel,
        grid=(KVH,),
        out_shape=(
            jax.ShapeDtypeStruct((rows, width), BF16),
            jax.ShapeDtypeStruct((rows, KVH * HD), BF16),
            jax.ShapeDtypeStruct((rows, KVH * HD), BF16),
            jax.ShapeDtypeStruct((shards, heads_out, shard_rows, HD), BF16),
        ),
        in_specs=[
            pl.BlockSpec(memory_space=pltpu.SMEM),
            pl.BlockSpec((rows, wide), column),
            pl.BlockSpec((1, wide), column),
            pl.BlockSpec((rows, wide), column),
            pl.BlockSpec((rows, HD), column),
            pl.BlockSpec((rows, HD), column),
            pl.BlockSpec((shards, 2, shard_rows, HD), lambda g: (0, g, 0, 0)),
        ],
        out_specs=(
            pl.BlockSpec((rows, wide), column),
            pl.BlockSpec((rows, HD), column),
            pl.BlockSpec((rows, HD), column),
            pl.BlockSpec((shards, heads_out, shard_rows, HD), lambda g: (0, 0, 0, 0)),
        ),
        scratch_shapes=[
            pltpu.VMEM((KVH * GROUP, HD), F32),
            pltpu.VMEM((key_count, GROUP * rows), BF16),
            pltpu.VMEM((key_count, GROUP * rows), BF16),
            pltpu.VMEM((GROUP * rows, HD), BF16),
            pltpu.VMEM((GROUP * rows, HD), BF16),
        ],
        compiler_params=pltpu.CompilerParams(
            dimension_semantics=("arbitrary",), vmem_limit_bytes=48 * 1024 * 1024
        ),
        cost_estimate=pl.CostEstimate(
            flops=10 * rows * width * key_count,
            transcendentals=rows * width // HD * key_count,
            bytes_accessed=8 * 1024 * 1024,
        ),
    )(length, queries, bias, cotangent, resp_keys, resp_values, gathered)


def spread(block, axis):
    copies = jnp.broadcast_to(block[None], (lax.axis_size(axis), *block.shape))
    return lax.all_to_all(copies, axis, 0, 0)


def body(
    prefix_keys, prefix_values, resp_queries, resp_keys, resp_values, query_bias, out_grad, lengths
):
    shard_rows = prefix_keys.shape[1]
    rows, width = resp_queries.shape[2:]
    shard = jnp.stack(
        [
            prefix_keys[0].reshape(shard_rows, KVH, HD),
            prefix_values[0].reshape(shard_rows, KVH, HD),
        ],
        2,
    )
    shard = shard.reshape(shard_rows, 2 * KVH, HD).transpose(1, 0, 2)
    gathered = spread(shard, "resp")
    dq, drk, drv, partial = attend(
        lengths, resp_queries[0, 0], query_bias[None, :], out_grad[0, 0],
        resp_keys[0, 0], resp_values[0, 0], gathered,
    )
    summed = jnp.sum(lax.all_to_all(partial, "resp", 0, 0).astype(F32), 0)
    prefix = summed[: 2 * KVH].astype(BF16).reshape(KVH, 2, shard_rows, HD)
    prefix = prefix.transpose(1, 2, 0, 3).reshape(2, shard_rows, KVH * HD)
    bias = summed[2 * KVH, :6].reshape(3, 2, HD).sum(0)
    bias = jnp.sum(spread(bias, "prompt"), 0)
    bias = spread(bias, "resp").reshape(-1)[:width]
    count = lax.axis_size("prompt") * lax.axis_size("resp") * rows
    return (
        dq[None, None],
        drk[None, None],
        drv[None, None],
        prefix[:1],
        prefix[1:],
        bias / math.sqrt(count),
    )


def solution(mesh):
    return jax.shard_map(
        body,
        mesh=mesh,
        in_specs=(
            P("prompt", "resp", None),
            P("prompt", "resp", None),
            P("prompt", "resp", None, None),
            P("prompt", "resp", None, None),
            P("prompt", "resp", None, None),
            P(),
            P("prompt", "resp", None, None),
            P("prompt", "resp"),
        ),
        out_specs=(
            P("prompt", "resp", None, None),
            P("prompt", "resp", None, None),
            P("prompt", "resp", None, None),
            P("prompt", "resp", None),
            P("prompt", "resp", None),
            P(),
        ),
        check_vma=False,
    )
```

```python
import functools
import math

import jax
import jax.numpy as jnp
from jax import lax
from jax.experimental import pallas as pl
from jax.experimental.pallas import tpu as pltpu
from jax.sharding import Mesh, PartitionSpec as P

HD = 128
GROUP = 5
KVH = 4
HALVES = 2
PER = KVH // HALVES
SCALE = 1.0 / math.sqrt(HD)
LOG2E = 1.4426950408889634
F32 = jnp.float32
BF16 = jnp.bfloat16

PROMPT = ("yh", "x1", "x0", "core")
RESP = ("yl", "z2", "z1", "z0")
SIZES = (4, 2, 2, 2, 2, 2, 2, 2)
Z = ("z2", "z1", "z0")


def dot(a, b, a_dim, b_dim):
    return lax.dot_general(a, b, (((a_dim,), (b_dim,)), ((), ())), preferred_element_type=F32)


def two_terms(total):
    high = total.astype(BF16)
    return jnp.concatenate([high, (total - high.astype(F32)).astype(BF16)], 1)


def attend_kernel(
    part, length_ref, q_ref, bias_ref, do_ref, rk_ref, rv_ref, k_near, v_near, k_far, v_far, *refs
):
    (dq_ref, drk_ref, drv_ref, near_ref, far_ref, sums_ref, probs_s, dscores_s, q_s, do_s) = refs[-10:]
    group = pl.program_id(0)

    @pl.when(group == 0)
    def _():
        sums_ref[...] = refs[3][...] if part else jnp.zeros_like(sums_ref)

    length = length_ref[0, 0]
    rows = q_ref.shape[0]
    shards, shard_rows, _ = k_near.shape
    half = shards * shard_rows
    prefix = 2 * half
    keys = jnp.concatenate(
        [k_near[...].reshape(half, HD), k_far[...].reshape(half, HD), rk_ref[...]], 0
    )
    values = jnp.concatenate(
        [v_near[...].reshape(half, HD), v_far[...].reshape(half, HD), rv_ref[...]], 0
    )
    live = lax.broadcasted_iota(jnp.int32, (rows, HD), 0) < length
    key_at = lax.broadcasted_iota(jnp.int32, (rows, rows), 0)
    row_at = lax.broadcasted_iota(jnp.int32, (rows, rows), 1)
    visible = (key_at <= row_at) & (key_at < length)
    for head in range(GROUP):
        cols = slice(head * HD, (head + 1) * HD)
        span = slice(head * rows, (head + 1) * rows)
        q = (q_ref[:, cols].astype(F32) + bias_ref[:, cols]).astype(BF16)
        do = jnp.where(live, do_ref[:, cols].astype(F32), 0.0).astype(BF16)
        q_s[span, :] = q
        do_s[span, :] = do
        scores = dot(keys, q, 1, 1) * (SCALE * LOG2E)
        scores = jnp.concatenate(
            [scores[:prefix], jnp.where(visible, scores[prefix:], -jnp.inf)], 0
        )
        expd = jnp.exp2(scores - jnp.max(scores, 0, keepdims=True))
        inverse = 1.0 / jnp.sum(expd, 0, keepdims=True)
        probs = expd * inverse
        dprobs = dot(values, do, 1, 1)
        delta = jnp.sum(probs * dprobs, 0, keepdims=True)
        probs_s[:, span] = probs.astype(BF16)
        dscores_s[:, span] = (probs * (dprobs - delta) * SCALE).astype(BF16)
    dscores = dscores_s[...]
    dk = dot(dscores, q_s[...], 1, 0)
    dv = dot(probs_s[...], do_s[...], 1, 0)
    for block, at in ((dk, group), (dv, PER + group)):
        lanes = pl.ds(pl.multiple_of(at * HD, HD), HD)
        block = block[:prefix].astype(BF16).reshape(2, shards, shard_rows, HD)
        near_ref[:, :, lanes] = block[0]
        far_ref[:shards, :, lanes] = block[1]
    drk_ref[...] = dk[prefix:].astype(BF16)
    drv_ref[...] = dv[prefix:].astype(BF16)
    dq_t = dot(keys, dscores, 0, 0)
    for head in range(GROUP):
        dq = dq_t[:, head * rows : (head + 1) * rows].T
        dq_ref[:, head * HD : (head + 1) * HD] = dq.astype(BF16)
        row = part * PER * GROUP + group * GROUP + head
        sums_ref[pl.ds(row, 1), :] = jnp.sum(dq, 0, keepdims=True)

    if part == HALVES - 1:

        @pl.when(group == PER - 1)
        def _():
            far_ref[shards, :, : 2 * HD] = two_terms(sums_ref[...])
            far_ref[shards, :, 2 * HD :] = jnp.zeros((shard_rows, (2 * PER - 2) * HD), BF16)


def attend(part, length, queries, bias, cotangent, resp_keys, resp_values, near, far, before):
    rows, width = queries.shape
    shards, shard_rows, _ = near.shape
    key_count = 2 * shards * shard_rows + rows
    slots = shards + (part == HALVES - 1)
    wide = GROUP * HD
    column = lambda g: (0, part * PER + g)
    block = (shards, shard_rows, HD)
    whole = (shards, shard_rows, 2 * PER * HD)
    sums = pl.BlockSpec((shard_rows, HD), lambda g: (0, 0))
    return pl.pallas_call(
        functools.partial(attend_kernel, part),
        grid=(PER,),
        out_shape=(
            jax.ShapeDtypeStruct((rows, width), BF16),
            jax.ShapeDtypeStruct((rows, KVH * HD), BF16),
            jax.ShapeDtypeStruct((rows, KVH * HD), BF16),
            jax.ShapeDtypeStruct(whole, BF16),
            jax.ShapeDtypeStruct((slots, *whole[1:]), BF16),
            jax.ShapeDtypeStruct((shard_rows, HD), F32),
        ),
        in_specs=[
            pl.BlockSpec(memory_space=pltpu.SMEM),
            pl.BlockSpec((rows, wide), column),
            pl.BlockSpec((1, wide), column),
            pl.BlockSpec((rows, wide), column),
            pl.BlockSpec((rows, HD), column),
            pl.BlockSpec((rows, HD), column),
            pl.BlockSpec(block, lambda g: (0, 0, part * 2 * PER + g)),
            pl.BlockSpec(block, lambda g: (0, 0, part * 2 * PER + PER + g)),
            pl.BlockSpec(block, lambda g: (0, 0, g)),
            pl.BlockSpec(block, lambda g: (0, 0, PER + g)),
            *[pl.BlockSpec(memory_space=pl.ANY)] * 3 * part,
            *[sums] * part,
        ],
        out_specs=(
            pl.BlockSpec((rows, wide), column),
            pl.BlockSpec((rows, HD), column),
            pl.BlockSpec((rows, HD), column),
            pl.BlockSpec(whole, lambda g: (0, 0, 0)),
            pl.BlockSpec((slots, *whole[1:]), lambda g: (0, 0, 0)),
            sums,
        ),
        scratch_shapes=[
            pltpu.VMEM((key_count, GROUP * rows), BF16),
            pltpu.VMEM((key_count, GROUP * rows), BF16),
            pltpu.VMEM((GROUP * rows, HD), BF16),
            pltpu.VMEM((GROUP * rows, HD), BF16),
        ],
        input_output_aliases={10 + i: i for i in range(3 * part)},
        compiler_params=pltpu.CompilerParams(
            dimension_semantics=("arbitrary",), vmem_limit_bytes=32 * 1024 * 1024
        ),
        cost_estimate=pl.CostEstimate(
            flops=10 * rows * width * key_count // HALVES,
            transcendentals=rows * width // HD * key_count // HALVES,
            bytes_accessed=4 * 1024 * 1024,
        ),
    )(length, queries, bias, cotangent, resp_keys, resp_values, near, near, far, far, *before)


def pair_kernel(near_a, got_a, near_b, got_b, sums, out):
    wide = near_a.shape[2]
    shards = out.shape[0]
    out[:, :, :wide] = (near_a[...].astype(F32) + got_a[...].astype(F32)).astype(BF16)
    got = got_b[:shards].astype(F32)
    out[:, :, wide : 2 * wide] = (near_b[...].astype(F32) + got).astype(BF16)
    terms = two_terms(sums[...])
    for shard in range(shards):
        out[shard, :, 2 * wide :] = terms


def finish_kernel(got, dk_ref, dv_ref, sums_ref):
    lanes = PER * HD
    total = got[0].astype(F32)
    for shard in range(1, got.shape[0]):
        total = total + got[shard].astype(F32)
    for part in range(HALVES):
        for at, ref in enumerate((dk_ref, dv_ref)):
            start = (2 * part + at) * lanes
            ref[:, part * lanes : (part + 1) * lanes] = total[:, start : start + lanes].astype(BF16)
    sums = total[:, 4 * lanes : 4 * lanes + HD] + total[:, 4 * lanes + HD :]
    for shard in range(sums_ref.shape[0]):
        sums_ref[shard] = sums[: sums_ref.shape[1]]


def spread(block, axis):
    copies = jnp.broadcast_to(block[None], (lax.axis_size(axis), *block.shape))
    return lax.all_to_all(copies, axis, 0, 0)


def swap(block, axis):
    return lax.ppermute(block, axis, [(0, 1), (1, 0)])


def body(
    prefix_keys, prefix_values, resp_queries, resp_keys, resp_values, query_bias, out_grad, lengths
):
    rows, width = resp_queries.shape[2:]
    shard_rows = prefix_keys.shape[1]
    lanes = PER * HD
    shard = jnp.concatenate(
        [
            array[0][:, part * lanes : (part + 1) * lanes]
            for part in range(HALVES)
            for array in (prefix_keys, prefix_values)
        ],
        1,
    )
    near = spread(shard, Z)
    wide = 2 * lanes
    far = [swap(near[:, :, part * wide : (part + 1) * wide], "yl") for part in range(HALVES)]
    operands = (
        lengths, resp_queries[0, 0], query_bias[None, :], out_grad[0, 0],
        resp_keys[0, 0], resp_values[0, 0], near,
    )
    *outs, near_a, far_a, sums = attend(0, *operands, far[0], ())
    got_a = swap(far_a, "yl")
    dq, drk, drv, near_b, far_b, sums = attend(1, *operands, far[1], (*outs, sums))
    far_b, got_a = lax.optimization_barrier((far_b, got_a))
    got_b = swap(far_b, "yl")
    terms = got_b[-1, :, : 2 * HD].astype(F32)
    sums = sums + terms[:, :HD] + terms[:, HD:]
    sums = sums + swap(sums, "core")
    shards = near.shape[0]
    pairs = pl.pallas_call(
        pair_kernel,
        out_shape=jax.ShapeDtypeStruct((shards, shard_rows, 2 * wide + 2 * HD), BF16),
    )(near_a, got_a, near_b, got_b, sums)
    groups = ("yh", "x1", "x0")
    prefix_dk, prefix_dv, sums = pl.pallas_call(
        finish_kernel,
        out_shape=(
            jax.ShapeDtypeStruct((shard_rows, KVH * HD), BF16),
            jax.ShapeDtypeStruct((shard_rows, KVH * HD), BF16),
            jax.ShapeDtypeStruct((lax.axis_size(groups), KVH * GROUP, HD), F32),
        ),
    )(lax.all_to_all(pairs, Z, 0, 0))
    sums = jnp.sum(lax.all_to_all(sums, groups, 0, 0), 0).reshape(width)
    count = math.prod(SIZES) * rows
    return (
        dq[None, None],
        drk[None, None],
        drv[None, None],
        prefix_dk[None],
        prefix_dv[None],
        sums / math.sqrt(count),
    )


def solution(mesh):
    fine = Mesh(mesh.devices.reshape(SIZES), PROMPT + RESP)
    return jax.shard_map(
        body,
        mesh=fine,
        in_specs=(
            P(PROMPT, RESP, None),
            P(PROMPT, RESP, None),
            P(PROMPT, RESP, None, None),
            P(PROMPT, RESP, None, None),
            P(PROMPT, RESP, None, None),
            P(),
            P(PROMPT, RESP, None, None),
            P(PROMPT, RESP),
        ),
        out_specs=(
            P(PROMPT, RESP, None, None),
            P(PROMPT, RESP, None, None),
            P(PROMPT, RESP, None, None),
            P(PROMPT, RESP, None),
            P(PROMPT, RESP, None),
            P(),
        ),
        check_vma=False,
    )
```

```python
import functools
import math

import jax
import jax.numpy as jnp
from jax import lax
from jax.experimental import pallas as pl
from jax.experimental.pallas import tpu as pltpu
from jax.sharding import Mesh, PartitionSpec as P

HD = 128
GROUP = 5
KVH = 4
PER = KVH // 2
SCALE = 1.0 / math.sqrt(HD)
LOG2E = 1.4426950408889634
F32 = jnp.float32
BF16 = jnp.bfloat16

PROMPT = ("yh", "x1", "x0", "core")
RESP = ("yl", "z2", "z1", "z0")
SIZES = (4, 2, 2, 2, 2, 2, 2, 2)
Z = ("z2", "z1", "z0")


def dot(a, b, a_dim, b_dim):
    return lax.dot_general(a, b, (((a_dim,), (b_dim,)), ((), ())), preferred_element_type=F32)


def prepare_kernel(
    length_ref, q_hbm, bias_ref, do_hbm, rk_hbm, rv_hbm, qs_ref, dos_ref, rk_ref, rv_ref, q_s, do_s, arrived
):
    reads = [
        pltpu.make_async_copy(source, target, arrived.at[i])
        for i, (source, target) in enumerate(
            ((q_hbm, q_s), (do_hbm, do_s), (rk_hbm, rk_ref), (rv_hbm, rv_ref))
        )
    ]
    for read in reads:
        read.start()
    rows = q_s.shape[0]
    live = lax.broadcasted_iota(jnp.int32, (rows, HD), 0) < length_ref[0, 0]
    reads[0].wait()
    for head in range(KVH * GROUP):
        cols = slice(head * HD, (head + 1) * HD)
        span = slice(head % GROUP * rows, (head % GROUP + 1) * rows)
        bias = bias_ref[cols].reshape(1, HD)
        qs_ref[head // GROUP, span, :] = (q_s[:, cols].astype(F32) + bias).astype(BF16)
    reads[1].wait()
    for head in range(KVH * GROUP):
        cols = slice(head * HD, (head + 1) * HD)
        span = slice(head % GROUP * rows, (head % GROUP + 1) * rows)
        dos_ref[head // GROUP, span, :] = jnp.where(live, do_s[:, cols].astype(F32), 0.0).astype(BF16)
    reads[2].wait()
    reads[3].wait()


def prepared(length, queries, bias, cotangent, resp_keys, resp_values):
    rows = queries.shape[0]
    hbm = pl.BlockSpec(memory_space=pltpu.HBM)
    tall = jax.ShapeDtypeStruct((KVH, GROUP * rows, HD), BF16)
    own = jax.ShapeDtypeStruct(resp_keys.shape, BF16)
    return pl.pallas_call(
        prepare_kernel,
        out_shape=(tall, tall, own, own),
        in_specs=[
            pl.BlockSpec(memory_space=pltpu.SMEM),
            hbm,
            pl.BlockSpec(memory_space=pltpu.VMEM),
            hbm,
            hbm,
            hbm,
        ],
        scratch_shapes=[
            pltpu.VMEM(queries.shape, BF16),
            pltpu.VMEM(cotangent.shape, BF16),
            pltpu.SemaphoreType.DMA((4,)),
        ],
        compiler_params=pltpu.CompilerParams(vmem_limit_bytes=16 * 1024 * 1024),
        cost_estimate=pl.CostEstimate(
            flops=queries.size, transcendentals=0, bytes_accessed=4 * 1024 * 1024
        ),
    )(length, queries, bias, cotangent, resp_keys, resp_values)


def attend_kernel(part, length_ref, qs_ref, dos_ref, rk_ref, rv_ref, near_in, far_in, *refs):
    flat_ref, drk_ref, drv_ref, near_ref, far_ref, sums_ref, columns, probs_s, dscores_s = refs[-9:]
    group = pl.program_id(0)
    length = length_ref[0, 0]
    rows = rk_ref.shape[0]
    shards, shard_rows, _ = near_in.shape
    shard_rows //= 2
    half = shards * shard_rows
    prefix = 2 * half
    keys, values = (
        jnp.concatenate(
            [
                near_in[:, at : at + shard_rows, :].reshape(half, HD),
                far_in[:, at : at + shard_rows, :].reshape(half, HD),
                own[...],
            ],
            0,
        )
        for at, own in ((0, rk_ref), (shard_rows, rv_ref))
    )
    key_at = lax.broadcasted_iota(jnp.int32, (rows, rows), 0)
    row_at = lax.broadcasted_iota(jnp.int32, (rows, rows), 1)
    visible = (key_at <= row_at) & (key_at < length)
    for head in range(GROUP):
        span = slice(head * rows, (head + 1) * rows)
        scores = dot(keys, qs_ref[0, span, :], 1, 1) * (SCALE * LOG2E)
        scores = jnp.concatenate(
            [scores[:prefix], jnp.where(visible, scores[prefix:], -jnp.inf)], 0
        )
        expd = jnp.exp2(scores - jnp.max(scores, 0, keepdims=True))
        inverse = 1.0 / jnp.sum(expd, 0, keepdims=True)
        probs = expd * inverse
        dprobs = dot(values, dos_ref[0, span, :], 1, 1)
        delta = jnp.sum(probs * dprobs, 0, keepdims=True)
        probs_s[:, span] = probs.astype(BF16)
        dscores_s[:, span] = (probs * (dprobs - delta) * SCALE).astype(BF16)
    dscores = dscores_s[...]
    for at, left, right, own in (
        (0, dscores, qs_ref, drk_ref),
        (shard_rows, probs_s[...], dos_ref, drv_ref),
    ):
        grad = dot(left, right[0], 1, 0).astype(BF16)
        own[...] = grad[prefix:]
        halves = grad[:prefix].reshape(2, shards, shard_rows, HD)
        near_ref[:, at : at + shard_rows, :] = halves[0]
        far_ref[:, at : at + shard_rows, :] = halves[1]
    dq = dot(keys, dscores, 0, 0)
    flat_ref[0] = dq.astype(BF16)
    for head in range(GROUP):
        columns[group, :, head : head + 1] = jnp.sum(
            dq[:, head * rows : (head + 1) * rows], 1, keepdims=True
        )

    @pl.when(group == PER - 1)
    def _():
        at = part * PER * GROUP
        for step in range(PER):
            sums = columns[step].T[:GROUP]
            for copy in range(sums_ref.shape[0]):
                sums_ref[copy, at + step * GROUP : at + (step + 1) * GROUP, :] = sums
        if part:
            for copy in range(sums_ref.shape[0]):
                sums_ref[copy, :at, :] = refs[5][0, :at, :]


def attend(part, length, qs, dos, resp_keys, resp_values, near, far, before, copies):
    rows = resp_keys.shape[0]
    shards, both_rows, width = near.shape
    key_count = shards * both_rows + rows
    columns = qs.shape[1]
    group_at = lambda g: part * PER + g
    column = lambda g: (0, group_at(g))
    stacked = lambda g: (group_at(g), 0, 0)
    blocked = lambda g: (0, 0, group_at(g))
    block = (shards, both_rows, HD)
    sums = lambda count: pl.BlockSpec((count, KVH * GROUP, HD), lambda g: (0, 0, 0))
    tall = (1, columns, HD)
    flat = (1, HD, columns)
    return pl.pallas_call(
        functools.partial(attend_kernel, part),
        grid=(PER,),
        out_shape=(
            jax.ShapeDtypeStruct((KVH, *flat[1:]), BF16),
            *[jax.ShapeDtypeStruct((rows, width), BF16)] * 2,
            *[jax.ShapeDtypeStruct((shards, both_rows, width), BF16)] * 2,
            jax.ShapeDtypeStruct((copies, KVH * GROUP, HD), F32),
        ),
        in_specs=[
            pl.BlockSpec(memory_space=pltpu.SMEM),
            pl.BlockSpec(tall, stacked),
            pl.BlockSpec(tall, stacked),
            pl.BlockSpec((rows, HD), column),
            pl.BlockSpec((rows, HD), column),
            pl.BlockSpec(block, blocked),
            pl.BlockSpec(block, lambda g: (0, 0, g)),
            *[pl.BlockSpec(memory_space=pl.ANY)] * 5 * part,
            *[sums(1)] * part,
        ],
        out_specs=(
            pl.BlockSpec(flat, stacked),
            *[pl.BlockSpec((rows, HD), column)] * 2,
            *[pl.BlockSpec(block, blocked)] * 2,
            sums(copies),
        ),
        scratch_shapes=[
            pltpu.VMEM((PER, HD, HD), F32),
            pltpu.VMEM((key_count, columns), BF16),
            pltpu.VMEM((key_count, columns), BF16),
        ],
        input_output_aliases={7 + i: i for i in range(5 * part)},
        compiler_params=pltpu.CompilerParams(
            dimension_semantics=("arbitrary",), vmem_limit_bytes=32 * 1024 * 1024
        ),
        cost_estimate=pl.CostEstimate(
            flops=10 * PER * columns * key_count * HD,
            transcendentals=PER * columns * key_count,
            bytes_accessed=4 * 1024 * 1024,
        ),
    )(length, qs, dos, resp_keys, resp_values, near, far, *before)


def turn_kernel(flat_ref, out_ref):
    rows = out_ref.shape[0]
    for group in range(KVH):
        for head in range(GROUP):
            at = (group * GROUP + head) * HD
            out_ref[:, at : at + HD] = flat_ref[group, :, head * rows : (head + 1) * rows].T


def pair_kernel(near, got, sums, out):
    shards, both_rows, width = near.shape
    more = out.shape[1] - both_rows
    out[:, :both_rows, :] = (near[...].astype(F32) + got[...].astype(F32)).astype(BF16)
    total = sums[0]
    for copy in range(1, sums.shape[0]):
        total = total + sums[copy]
    total = jnp.concatenate([total, jnp.zeros((2 * more - total.shape[0], HD), F32)], 0)
    high = total.astype(BF16)
    low = (total - high.astype(F32)).astype(BF16)
    terms = jnp.concatenate([high[:more], high[more:], low[:more], low[more:]], 1)
    for shard in range(shards):
        out[shard, both_rows:, :] = terms


def finish_kernel(got, dk_ref, dv_ref, sums_ref):
    rows = dk_ref.shape[0]
    total = got[0].astype(F32)
    for shard in range(1, got.shape[0]):
        total = total + got[shard].astype(F32)
    dk_ref[...] = total[:rows].astype(BF16)
    dv_ref[...] = total[rows : 2 * rows].astype(BF16)
    terms = total[2 * rows :, : 2 * HD] + total[2 * rows :, 2 * HD :]
    sums = jnp.concatenate([terms[:, :HD], terms[:, HD:]], 0)[: sums_ref.shape[1]]
    for copy in range(sums_ref.shape[0]):
        sums_ref[copy] = sums


def small_call(kernel, out_shape, *operands):
    return pl.pallas_call(
        kernel,
        out_shape=out_shape,
        compiler_params=pltpu.CompilerParams(vmem_limit_bytes=8 * 1024 * 1024),
    )(*operands)


def spread(block, axis):
    copies = jnp.broadcast_to(block[None], (lax.axis_size(axis), *block.shape))
    return lax.all_to_all(copies, axis, 0, 0)


def swap(block, axis):
    return lax.ppermute(block, axis, [(0, 1), (1, 0)])


def body(
    prefix_keys, prefix_values, resp_queries, resp_keys, resp_values, query_bias, out_grad, lengths
):
    rows, width = resp_queries.shape[2:]
    shard_rows, kv_width = prefix_keys.shape[1:]
    near = spread(jnp.concatenate([prefix_keys[0], prefix_values[0]], 0), Z)
    qs, dos, rk, rv = prepared(
        lengths, resp_queries[0, 0], query_bias, out_grad[0, 0], resp_keys[0, 0], resp_values[0, 0]
    )
    near, qs, dos, rk, rv = lax.optimization_barrier((near, qs, dos, rk, rv))
    operands = (lengths, qs, dos, rk, rv, near)
    wide = PER * HD
    far_a = swap(near[:, :, :wide], "yl")
    far_a, near_b = lax.optimization_barrier((far_a, near[:, :, wide:]))
    far_b = swap(near_b, "yl")
    first, last = ("x1", "x0", "core"), ("yh", "yl")
    held = attend(0, *operands, far_a, (), 1)
    flat, drk, drv, mine, others, sums = attend(1, *operands, far_b, held, lax.axis_size(first))
    got = swap(others, "yl")
    sums = lax.all_to_all(sums, first, 0, 0)
    pairs = small_call(
        pair_kernel,
        jax.ShapeDtypeStruct((near.shape[0], 2 * shard_rows + 16, kv_width), BF16),
        mine, got, sums,
    )
    pairs, flat = lax.optimization_barrier((pairs, flat))
    dq = small_call(turn_kernel, jax.ShapeDtypeStruct((rows, width), BF16), flat)
    prefix_dk, prefix_dv, sums = small_call(
        finish_kernel,
        (
            jax.ShapeDtypeStruct((shard_rows, kv_width), BF16),
            jax.ShapeDtypeStruct((shard_rows, kv_width), BF16),
            jax.ShapeDtypeStruct((lax.axis_size(last), KVH * GROUP, HD), F32),
        ),
        lax.all_to_all(pairs, Z, 0, 0),
    )
    sums = jnp.sum(lax.all_to_all(sums, last, 0, 0), 0).reshape(width)
    return (
        dq[None, None],
        drk[None, None],
        drv[None, None],
        prefix_dk[None],
        prefix_dv[None],
        sums / math.sqrt(math.prod(SIZES) * rows),
    )


def solution(mesh):
    fine = Mesh(mesh.devices.reshape(SIZES), PROMPT + RESP)
    return jax.shard_map(
        body,
        mesh=fine,
        in_specs=(
            P(PROMPT, RESP, None),
            P(PROMPT, RESP, None),
            P(PROMPT, RESP, None, None),
            P(PROMPT, RESP, None, None),
            P(PROMPT, RESP, None, None),
            P(),
            P(PROMPT, RESP, None, None),
            P(PROMPT, RESP),
        ),
        out_specs=(
            P(PROMPT, RESP, None, None),
            P(PROMPT, RESP, None, None),
            P(PROMPT, RESP, None, None),
            P(PROMPT, RESP, None),
            P(PROMPT, RESP, None),
            P(),
        ),
        check_vma=False,
    )
```

```python
import functools
import math

import jax
import jax.numpy as jnp
from jax import lax
from jax.experimental import pallas as pl
from jax.experimental.pallas import tpu as pltpu
from jax.sharding import Mesh, PartitionSpec as P

HD = 128
GROUP = 5
KVH = 4
SCALE = 1.0 / math.sqrt(HD)
LOG2E = 1.4426950408889634
F32 = jnp.float32
BF16 = jnp.bfloat16

PROMPT = ("yh", "x1", "x0", "core")
RESP = ("yl", "z2", "z1", "z0")
SIZES = (4, 2, 2, 2, 2, 2, 2, 2)
Z = ("z2", "z1", "z0")


def dot(a, b, a_dim, b_dim):
    return lax.dot_general(a, b, (((a_dim,), (b_dim,)), ((), ())), preferred_element_type=F32)


def prepare_kernel(
    length_ref, q_hbm, bias_ref, do_hbm, rk_hbm, rv_hbm, qs_ref, dos_ref, rk_ref, rv_ref, q_s, do_s, arrived
):
    reads = [
        pltpu.make_async_copy(source, target, arrived.at[i])
        for i, (source, target) in enumerate(
            ((q_hbm, q_s), (do_hbm, do_s), (rk_hbm, rk_ref), (rv_hbm, rv_ref))
        )
    ]
    for read in reads:
        read.start()
    rows = q_s.shape[0]
    live = lax.broadcasted_iota(jnp.int32, (rows, HD), 0) < length_ref[0, 0]
    reads[0].wait()
    for head in range(KVH * GROUP):
        cols = slice(head * HD, (head + 1) * HD)
        span = slice(head % GROUP * rows, (head % GROUP + 1) * rows)
        bias = bias_ref[cols].reshape(1, HD)
        qs_ref[head // GROUP, span, :] = (q_s[:, cols].astype(F32) + bias).astype(BF16)
    reads[1].wait()
    for head in range(KVH * GROUP):
        cols = slice(head * HD, (head + 1) * HD)
        span = slice(head % GROUP * rows, (head % GROUP + 1) * rows)
        dos_ref[head // GROUP, span, :] = jnp.where(live, do_s[:, cols].astype(F32), 0.0).astype(BF16)
    reads[2].wait()
    reads[3].wait()


def prepared(length, queries, bias, cotangent, resp_keys, resp_values):
    rows = queries.shape[0]
    hbm = pl.BlockSpec(memory_space=pltpu.HBM)
    tall = jax.ShapeDtypeStruct((KVH, GROUP * rows, HD), BF16)
    own = jax.ShapeDtypeStruct(resp_keys.shape, BF16)
    return pl.pallas_call(
        prepare_kernel,
        out_shape=(tall, tall, own, own),
        in_specs=[
            pl.BlockSpec(memory_space=pltpu.SMEM),
            hbm,
            pl.BlockSpec(memory_space=pltpu.VMEM),
            hbm,
            hbm,
            hbm,
        ],
        scratch_shapes=[
            pltpu.VMEM(queries.shape, BF16),
            pltpu.VMEM(cotangent.shape, BF16),
            pltpu.SemaphoreType.DMA((4,)),
        ],
        compiler_params=pltpu.CompilerParams(vmem_limit_bytes=16 * 1024 * 1024),
        cost_estimate=pl.CostEstimate(
            flops=queries.size, transcendentals=0, bytes_accessed=4 * 1024 * 1024
        ),
    )(length, queries, bias, cotangent, resp_keys, resp_values)


def attend_kernel(
    length_ref, qs_ref, dos_ref, rk_ref, rv_ref, near_in, far_in,
    flat_ref, drk_ref, drv_ref, near_ref, far_ref, sums_ref, columns, probs_s, dscores_s,
):
    group = pl.program_id(0)
    length = length_ref[0, 0]
    rows = rk_ref.shape[0]
    shards, both_rows, _ = near_in.shape
    shard_rows = both_rows // 2
    half = shards * shard_rows
    prefix = 2 * half
    keys, values = (
        jnp.concatenate(
            [
                near_in[:, at : at + shard_rows, :].reshape(half, HD),
                far_in[:, at : at + shard_rows, :].reshape(half, HD),
                own[...],
            ],
            0,
        )
        for at, own in ((0, rk_ref), (shard_rows, rv_ref))
    )
    key_at = lax.broadcasted_iota(jnp.int32, (rows, rows), 0)
    row_at = lax.broadcasted_iota(jnp.int32, (rows, rows), 1)
    visible = (key_at <= row_at) & (key_at < length)
    for head in range(GROUP):
        span = slice(head * rows, (head + 1) * rows)
        scores = dot(keys, qs_ref[0, span, :], 1, 1)
        scores = jnp.concatenate(
            [scores[:prefix], jnp.where(visible, scores[prefix:], -jnp.inf)], 0
        )
        top = jnp.max(scores, 0, keepdims=True) * (SCALE * LOG2E)
        expd = jnp.exp2(scores * (SCALE * LOG2E) - top)
        inverse = 1.0 / jnp.sum(expd, 0, keepdims=True)
        dprobs = dot(values, dos_ref[0, span, :], 1, 1)
        delta = jnp.sum(expd * dprobs, 0, keepdims=True) * inverse
        probs_s[:, span] = (expd * inverse).astype(BF16)
        dscores_s[:, span] = (expd * ((dprobs - delta) * (inverse * SCALE))).astype(BF16)
    dscores = dscores_s[...]
    for at, left, right, own in (
        (0, dscores, qs_ref, drk_ref),
        (shard_rows, probs_s[...], dos_ref, drv_ref),
    ):
        grad = dot(left, right[0], 1, 0).astype(BF16)
        own[...] = grad[prefix:]
        halves = grad[:prefix].reshape(2, shards, shard_rows, HD)
        near_ref[:, at : at + shard_rows, :] = halves[0]
        far_ref[:, at : at + shard_rows, :] = halves[1]
    dq = dot(keys, dscores, 0, 0)
    flat_ref[0] = dq.astype(BF16)
    for head in range(GROUP):
        columns[group, :, head : head + 1] = jnp.sum(
            dq[:, head * rows : (head + 1) * rows], 1, keepdims=True
        )

    @pl.when(group == KVH - 1)
    def _():
        for step in range(KVH):
            sums = columns[step].T[:GROUP]
            for copy in range(sums_ref.shape[0]):
                sums_ref[copy, step * GROUP : (step + 1) * GROUP, :] = sums


def attend(length, qs, dos, resp_keys, resp_values, near, far, copies):
    rows, width = resp_keys.shape
    shards, both_rows, _ = near.shape
    key_count = shards * both_rows + rows
    columns = qs.shape[1]
    stacked = lambda g: (g, 0, 0)
    own = pl.BlockSpec((rows, HD), lambda g: (0, g))
    block = pl.BlockSpec((shards, both_rows, HD), lambda g: (0, 0, g))
    tall = pl.BlockSpec((1, columns, HD), stacked)
    sums = (copies, KVH * GROUP, HD)
    return pl.pallas_call(
        attend_kernel,
        grid=(KVH,),
        out_shape=(
            jax.ShapeDtypeStruct((KVH, HD, columns), BF16),
            *[jax.ShapeDtypeStruct((rows, width), BF16)] * 2,
            *[jax.ShapeDtypeStruct((shards, both_rows, width), BF16)] * 2,
            jax.ShapeDtypeStruct(sums, F32),
        ),
        in_specs=[pl.BlockSpec(memory_space=pltpu.SMEM), tall, tall, own, own, block, block],
        out_specs=(
            pl.BlockSpec((1, HD, columns), stacked),
            own,
            own,
            block,
            block,
            pl.BlockSpec(sums, lambda g: (0, 0, 0)),
        ),
        scratch_shapes=[
            pltpu.VMEM((KVH, HD, HD), F32),
            pltpu.VMEM((key_count, columns), BF16),
            pltpu.VMEM((key_count, columns), BF16),
        ],
        compiler_params=pltpu.CompilerParams(
            dimension_semantics=("arbitrary",), vmem_limit_bytes=32 * 1024 * 1024
        ),
        cost_estimate=pl.CostEstimate(
            flops=10 * KVH * columns * key_count * HD,
            transcendentals=KVH * columns * key_count,
            bytes_accessed=6 * 1024 * 1024,
        ),
    )(length, qs, dos, resp_keys, resp_values, near, far)


def turn_kernel(flat_ref, out_ref):
    rows = out_ref.shape[0]
    for group in range(KVH):
        for head in range(GROUP):
            at = (group * GROUP + head) * HD
            out_ref[:, at : at + HD] = flat_ref[group, :, head * rows : (head + 1) * rows].T


def total_kernel(got, out):
    total = got[0]
    for copy in range(1, got.shape[0]):
        total = total + got[copy]
    for copy in range(out.shape[0]):
        out[copy] = total


def pair_kernel(near, got, sums, out):
    shards, both_rows, width = near.shape
    more = out.shape[1] - both_rows
    out[:, :both_rows, :] = (near[...].astype(F32) + got[...].astype(F32)).astype(BF16)
    total = sums[0]
    for copy in range(1, sums.shape[0]):
        total = total + sums[copy]
    total = jnp.concatenate([total, jnp.zeros((2 * more - total.shape[0], HD), F32)], 0)
    high = total.astype(BF16)
    low = (total - high.astype(F32)).astype(BF16)
    terms = jnp.concatenate([high[:more], high[more:], low[:more], low[more:]], 1)
    for shard in range(shards):
        out[shard, both_rows:, :] = terms


def finish_kernel(divisor, got, dk_ref, dv_ref, sums_ref):
    rows = dk_ref.shape[0]
    total = got[0].astype(F32)
    for shard in range(1, got.shape[0]):
        total = total + got[shard].astype(F32)
    dk_ref[...] = total[:rows].astype(BF16)
    dv_ref[...] = total[rows : 2 * rows].astype(BF16)
    terms = total[2 * rows :, : 2 * HD] + total[2 * rows :, 2 * HD :]
    sums = jnp.concatenate([terms[:, :HD], terms[:, HD:]], 0)[: sums_ref.shape[0]]
    sums_ref[...] = sums / divisor


def small_call(kernel, out_shape, *operands):
    return pl.pallas_call(
        kernel,
        out_shape=out_shape,
        compiler_params=pltpu.CompilerParams(vmem_limit_bytes=8 * 1024 * 1024),
    )(*operands)


def spread(block, axis):
    copies = jnp.broadcast_to(block[None], (lax.axis_size(axis), *block.shape))
    return lax.all_to_all(copies, axis, 0, 0)


def swap(block, axis):
    return lax.ppermute(block, axis, [(0, 1), (1, 0)])


def body(
    prefix_keys, prefix_values, resp_queries, resp_keys, resp_values, query_bias, out_grad, lengths
):
    rows, width = resp_queries.shape[2:]
    shard_rows, kv_width = prefix_keys.shape[1:]
    near = spread(jnp.concatenate([prefix_keys[0], prefix_values[0]], 0), Z)
    qs, dos, rk, rv = prepared(
        lengths, resp_queries[0, 0], query_bias, out_grad[0, 0], resp_keys[0, 0], resp_values[0, 0]
    )
    first, second = ("x1", "x0", "core"), ("yh", "yl")
    flat, drk, drv, mine, others, sums = attend(
        lengths, qs, dos, rk, rv, near, swap(near, "yl"), lax.axis_size(first)
    )
    got = swap(others, "yl")
    sums = small_call(
        total_kernel,
        jax.ShapeDtypeStruct((lax.axis_size(second), *sums.shape[1:]), F32),
        lax.all_to_all(sums, first, 0, 0),
    )
    pairs = small_call(
        pair_kernel,
        jax.ShapeDtypeStruct((near.shape[0], 2 * shard_rows + 16, kv_width), BF16),
        mine, got, lax.all_to_all(sums, second, 0, 0),
    )
    pairs, flat = lax.optimization_barrier((pairs, flat))
    dq = small_call(turn_kernel, jax.ShapeDtypeStruct((rows, width), BF16), flat)
    summed, dq = lax.optimization_barrier((lax.all_to_all(pairs, Z, 0, 0), dq))
    prefix_dk, prefix_dv, sums = small_call(
        functools.partial(finish_kernel, math.sqrt(math.prod(SIZES) * rows)),
        (
            jax.ShapeDtypeStruct((shard_rows, kv_width), BF16),
            jax.ShapeDtypeStruct((shard_rows, kv_width), BF16),
            jax.ShapeDtypeStruct((KVH * GROUP, HD), F32),
        ),
        summed,
    )
    return (
        dq[None, None],
        drk[None, None],
        drv[None, None],
        prefix_dk[None],
        prefix_dv[None],
        sums.reshape(width),
    )


def solution(mesh):
    fine = Mesh(mesh.devices.reshape(SIZES), PROMPT + RESP)
    return jax.shard_map(
        body,
        mesh=fine,
        in_specs=(
            P(PROMPT, RESP, None),
            P(PROMPT, RESP, None),
            P(PROMPT, RESP, None, None),
            P(PROMPT, RESP, None, None),
            P(PROMPT, RESP, None, None),
            P(),
            P(PROMPT, RESP, None, None),
            P(PROMPT, RESP),
        ),
        out_specs=(
            P(PROMPT, RESP, None, None),
            P(PROMPT, RESP, None, None),
            P(PROMPT, RESP, None, None),
            P(PROMPT, RESP, None),
            P(PROMPT, RESP, None),
            P(),
        ),
        check_vma=False,
    )
```

```python
import functools
import math

import jax
import jax.numpy as jnp
from jax import lax
from jax.experimental import pallas as pl
from jax.experimental.pallas import tpu as pltpu
from jax.sharding import Mesh, PartitionSpec as P

HD = 128
GROUP = 5
KVH = 4
SCALE = 1.0 / math.sqrt(HD)
LOG2E = 1.4426950408889634
F32 = jnp.float32
BF16 = jnp.bfloat16

PROMPT = ("yh", "x1", "x0", "core")
RESP = ("yl", "z2", "z1", "z0")
SIZES = (4, 2, 2, 2, 2, 2, 2, 2)
Z = ("z2", "z1", "z0")


def dot(a, b, a_dim, b_dim):
    return lax.dot_general(a, b, (((a_dim,), (b_dim,)), ((), ())), preferred_element_type=F32)


def prepare_kernel(
    length_ref, q_hbm, bias_ref, do_hbm, rk_hbm, rv_hbm, qs_ref, dos_ref, rk_ref, rv_ref, q_s, do_s, arrived
):
    reads = [
        pltpu.make_async_copy(source, target, arrived.at[i])
        for i, (source, target) in enumerate(
            ((q_hbm, q_s), (do_hbm, do_s), (rk_hbm, rk_ref), (rv_hbm, rv_ref))
        )
    ]
    for read in reads:
        read.start()
    rows = q_s.shape[0]
    live = lax.broadcasted_iota(jnp.int32, (rows, HD), 0) < length_ref[0, 0]
    reads[0].wait()
    for head in range(KVH * GROUP):
        cols = slice(head * HD, (head + 1) * HD)
        span = slice(head % GROUP * rows, (head % GROUP + 1) * rows)
        bias = bias_ref[cols].reshape(1, HD)
        qs_ref[head // GROUP, span, :] = (q_s[:, cols].astype(F32) + bias).astype(BF16)
    reads[1].wait()
    for head in range(KVH * GROUP):
        cols = slice(head * HD, (head + 1) * HD)
        span = slice(head % GROUP * rows, (head % GROUP + 1) * rows)
        dos_ref[head // GROUP, span, :] = jnp.where(live, do_s[:, cols].astype(F32), 0.0).astype(BF16)
    reads[2].wait()
    reads[3].wait()


def prepared(length, queries, bias, cotangent, resp_keys, resp_values):
    rows = queries.shape[0]
    hbm = pl.BlockSpec(memory_space=pltpu.HBM)
    tall = jax.ShapeDtypeStruct((KVH, GROUP * rows, HD), BF16)
    own = jax.ShapeDtypeStruct(resp_keys.shape, BF16)
    return pl.pallas_call(
        prepare_kernel,
        out_shape=(tall, tall, own, own),
        in_specs=[
            pl.BlockSpec(memory_space=pltpu.SMEM),
            hbm,
            pl.BlockSpec(memory_space=pltpu.VMEM),
            hbm,
            hbm,
            hbm,
        ],
        scratch_shapes=[
            pltpu.VMEM(queries.shape, BF16),
            pltpu.VMEM(cotangent.shape, BF16),
            pltpu.SemaphoreType.DMA((4,)),
        ],
        compiler_params=pltpu.CompilerParams(vmem_limit_bytes=16 * 1024 * 1024),
        cost_estimate=pl.CostEstimate(
            flops=queries.size, transcendentals=0, bytes_accessed=4 * 1024 * 1024
        ),
    )(length, queries, bias, cotangent, resp_keys, resp_values)


def near_kernel(
    length_ref, qs_ref, dos_ref, rk_ref, rv_ref, near_in, expd_ref, dprobs_ref, stats_ref
):
    length = length_ref[0, 0]
    rows = rk_ref.shape[0]
    shards, both_rows, _ = near_in.shape
    shard_rows = both_rows // 2
    half = shards * shard_rows
    key_at = lax.broadcasted_iota(jnp.int32, (rows, rows), 0)
    row_at = lax.broadcasted_iota(jnp.int32, (rows, rows), 1)
    visible = (key_at <= row_at) & (key_at < length)
    for group in range(KVH):
        cols = slice(group * HD, (group + 1) * HD)
        keys, values = (
            jnp.concatenate(
                [near_in[:, at : at + shard_rows, cols].reshape(half, HD), own[:, cols]], 0
            )
            for at, own in ((0, rk_ref), (shard_rows, rv_ref))
        )
        for head in range(GROUP):
            span = slice(head * rows, (head + 1) * rows)
            scores = dot(keys, qs_ref[group, span, :], 1, 1)
            scores = jnp.concatenate(
                [scores[:half], jnp.where(visible, scores[half:], -jnp.inf)], 0
            )
            top = jnp.max(scores, 0, keepdims=True) * (SCALE * LOG2E)
            expd = jnp.exp2(scores * (SCALE * LOG2E) - top)
            dprobs = dot(values, dos_ref[group, span, :], 1, 1)
            expd_ref[group, :, span] = expd
            dprobs_ref[group, :, span] = dprobs
            stats_ref[group, 0:1, span] = top
            stats_ref[group, 1:2, span] = jnp.sum(expd, 0, keepdims=True)
            stats_ref[group, 2:3, span] = jnp.sum(expd * dprobs, 0, keepdims=True)


def near_scores(length, qs, dos, resp_keys, resp_values, near):
    shards, both_rows, _ = near.shape
    columns = qs.shape[1]
    square = (KVH, shards * both_rows // 2 + resp_keys.shape[0], columns)
    vmem = pl.BlockSpec(memory_space=pltpu.VMEM)
    return pl.pallas_call(
        near_kernel,
        out_shape=(
            jax.ShapeDtypeStruct(square, F32),
            jax.ShapeDtypeStruct(square, F32),
            jax.ShapeDtypeStruct((KVH, 8, columns), F32),
        ),
        in_specs=[pl.BlockSpec(memory_space=pltpu.SMEM), *[vmem] * 5],
        out_specs=(vmem,) * 3,
        compiler_params=pltpu.CompilerParams(vmem_limit_bytes=16 * 1024 * 1024),
        cost_estimate=pl.CostEstimate(
            flops=4 * KVH * columns * square[1] * HD,
            transcendentals=KVH * columns * square[1],
            bytes_accessed=2 * 1024 * 1024,
        ),
    )(length, qs, dos, resp_keys, resp_values, near)


def attend_kernel(
    qs_ref, dos_ref, rk_ref, near_in, far_in, expd_in, dprobs_in, stats_in,
    flat_ref, drk_ref, drv_ref, near_ref, far_ref, sums_ref, probs_s, dscores_s,
):
    rows = rk_ref.shape[0]
    shards, both_rows, _ = near_in.shape
    shard_rows = both_rows // 2
    half = shards * shard_rows
    first = half + rows
    for group in range(KVH):
        cols = slice(group * HD, (group + 1) * HD)
        far_keys = far_in[:, :shard_rows, cols].reshape(half, HD)
        far_values = far_in[:, shard_rows:, cols].reshape(half, HD)
        for head in range(GROUP):
            span = slice(head * rows, (head + 1) * rows)
            scores = dot(far_keys, qs_ref[group, span, :], 1, 1)
            near_top = stats_in[group, 0:1, span]
            top = jnp.max(scores, 0, keepdims=True) * (SCALE * LOG2E)
            top = jnp.maximum(top, near_top)
            shrink = jnp.exp2(near_top - top)
            expd = jnp.exp2(scores * (SCALE * LOG2E) - top)
            total = stats_in[group, 1:2, span] * shrink + jnp.sum(expd, 0, keepdims=True)
            inverse = 1.0 / total
            dprobs = dot(far_values, dos_ref[group, span, :], 1, 1)
            delta = stats_in[group, 2:3, span] * shrink + jnp.sum(expd * dprobs, 0, keepdims=True)
            delta = delta * inverse
            probs_s[group, first:, span] = (expd * inverse).astype(BF16)
            dscores_s[group, first:, span] = (
                expd * ((dprobs - delta) * (inverse * SCALE))
            ).astype(BF16)
            factor = shrink * inverse
            expd = expd_in[group, :, span]
            dprobs = dprobs_in[group, :, span]
            probs_s[group, :first, span] = (expd * factor).astype(BF16)
            dscores_s[group, :first, span] = (
                expd * ((dprobs - delta) * (factor * SCALE))
            ).astype(BF16)
        dscores = dscores_s[group]
        for at, left, right, own in (
            (0, dscores, qs_ref, drk_ref),
            (shard_rows, probs_s[group], dos_ref, drv_ref),
        ):
            grad = dot(left, right[group], 1, 0).astype(BF16)
            own[:, cols] = grad[half:first]
            for ref, part in ((near_ref, grad[:half]), (far_ref, grad[first:])):
                ref[:, at : at + shard_rows, cols] = part.reshape(shards, shard_rows, HD)
        near_keys = near_in[:, :shard_rows, cols].reshape(half, HD)
        keys = jnp.concatenate([near_keys, rk_ref[:, cols], far_keys], 0)
        dq = dot(keys, dscores, 0, 0)
        flat_ref[group] = dq.astype(BF16)
        columns = [
            jnp.sum(dq[:, head * rows : (head + 1) * rows], 1, keepdims=True)
            for head in range(GROUP)
        ]
        columns.append(jnp.zeros((HD, HD - GROUP), F32))
        sums = jnp.concatenate(columns, 1).T[:GROUP]
        for copy in range(sums_ref.shape[0]):
            sums_ref[copy, group * GROUP : (group + 1) * GROUP, :] = sums


def attend(qs, dos, resp_keys, near, far, expd, dprobs, stats, copies):
    rows, width = resp_keys.shape
    shards, both_rows, _ = near.shape
    key_count = shards * both_rows + rows
    columns = qs.shape[1]
    vmem = pl.BlockSpec(memory_space=pltpu.VMEM)
    return pl.pallas_call(
        attend_kernel,
        out_shape=(
            jax.ShapeDtypeStruct((KVH, HD, columns), BF16),
            *[jax.ShapeDtypeStruct((rows, width), BF16)] * 2,
            *[jax.ShapeDtypeStruct((shards, both_rows, width), BF16)] * 2,
            jax.ShapeDtypeStruct((copies, KVH * GROUP, HD), F32),
        ),
        in_specs=[vmem] * 8,
        out_specs=(vmem,) * 6,
        scratch_shapes=[pltpu.VMEM((KVH, key_count, columns), BF16)] * 2,
        compiler_params=pltpu.CompilerParams(vmem_limit_bytes=32 * 1024 * 1024),
        cost_estimate=pl.CostEstimate(
            flops=8 * KVH * columns * key_count * HD,
            transcendentals=KVH * columns * key_count // 2,
            bytes_accessed=6 * 1024 * 1024,
        ),
    )(qs, dos, resp_keys, near, far, expd, dprobs, stats)


def turn_kernel(flat_ref, out_ref):
    rows = out_ref.shape[0]
    for group in range(KVH):
        for head in range(GROUP):
            at = (group * GROUP + head) * HD
            out_ref[:, at : at + HD] = flat_ref[group, :, head * rows : (head + 1) * rows].T


def total_kernel(got, out):
    total = got[0]
    for copy in range(1, got.shape[0]):
        total = total + got[copy]
    for copy in range(out.shape[0]):
        out[copy] = total


def pair_kernel(near, got, sums, out):
    shards, both_rows, width = near.shape
    more = out.shape[1] - both_rows
    out[:, :both_rows, :] = (near[...].astype(F32) + got[...].astype(F32)).astype(BF16)
    total = sums[0]
    for copy in range(1, sums.shape[0]):
        total = total + sums[copy]
    total = jnp.concatenate([total, jnp.zeros((2 * more - total.shape[0], HD), F32)], 0)
    high = total.astype(BF16)
    low = (total - high.astype(F32)).astype(BF16)
    terms = jnp.concatenate([high[:more], high[more:], low[:more], low[more:]], 1)
    for shard in range(shards):
        out[shard, both_rows:, :] = terms


def finish_kernel(divisor, got, dk_ref, dv_ref, sums_ref):
    rows = dk_ref.shape[0]
    total = got[0].astype(F32)
    for shard in range(1, got.shape[0]):
        total = total + got[shard].astype(F32)
    dk_ref[...] = total[:rows].astype(BF16)
    dv_ref[...] = total[rows : 2 * rows].astype(BF16)
    terms = total[2 * rows :, : 2 * HD] + total[2 * rows :, 2 * HD :]
    sums = jnp.concatenate([terms[:, :HD], terms[:, HD:]], 0)[: sums_ref.shape[0]]
    sums_ref[...] = sums / divisor


def small_call(kernel, out_shape, *operands):
    return pl.pallas_call(
        kernel,
        out_shape=out_shape,
        compiler_params=pltpu.CompilerParams(vmem_limit_bytes=8 * 1024 * 1024),
    )(*operands)


def spread(block, axis):
    copies = jnp.broadcast_to(block[None], (lax.axis_size(axis), *block.shape))
    return lax.all_to_all(copies, axis, 0, 0)


def swap(block, axis):
    return lax.ppermute(block, axis, [(0, 1), (1, 0)])


def body(
    prefix_keys, prefix_values, resp_queries, resp_keys, resp_values, query_bias, out_grad, lengths
):
    rows, width = resp_queries.shape[2:]
    shard_rows, kv_width = prefix_keys.shape[1:]
    near = spread(jnp.concatenate([prefix_keys[0], prefix_values[0]], 0), Z)
    qs, dos, rk, rv = prepared(
        lengths, resp_queries[0, 0], query_bias, out_grad[0, 0], resp_keys[0, 0], resp_values[0, 0]
    )
    first, second = ("x1", "x0", "core"), ("yh", "yl")
    far = swap(near, "yl")
    held = near_scores(lengths, qs, dos, rk, rv, near)
    flat, drk, drv, mine, others, sums = attend(
        qs, dos, rk, near, far, *held, lax.axis_size(first)
    )
    got = swap(others, "yl")
    sums = small_call(
        total_kernel,
        jax.ShapeDtypeStruct((lax.axis_size(second), *sums.shape[1:]), F32),
        lax.all_to_all(sums, first, 0, 0),
    )
    sums, flat = lax.optimization_barrier((sums, flat))
    dq = small_call(turn_kernel, jax.ShapeDtypeStruct((rows, width), BF16), flat)
    sums, dq = lax.optimization_barrier((lax.all_to_all(sums, second, 0, 0), dq))
    pairs = small_call(
        pair_kernel,
        jax.ShapeDtypeStruct((near.shape[0], 2 * shard_rows + 16, kv_width), BF16),
        mine, got, sums,
    )
    summed = lax.all_to_all(pairs, Z, 0, 0)
    prefix_dk, prefix_dv, sums = small_call(
        functools.partial(finish_kernel, math.sqrt(math.prod(SIZES) * rows)),
        (
            jax.ShapeDtypeStruct((shard_rows, kv_width), BF16),
            jax.ShapeDtypeStruct((shard_rows, kv_width), BF16),
            jax.ShapeDtypeStruct((KVH * GROUP, HD), F32),
        ),
        summed,
    )
    return (
        dq[None, None],
        drk[None, None],
        drv[None, None],
        prefix_dk[None],
        prefix_dv[None],
        sums.reshape(width),
    )


def solution(mesh):
    fine = Mesh(mesh.devices.reshape(SIZES), PROMPT + RESP)
    return jax.shard_map(
        body,
        mesh=fine,
        in_specs=(
            P(PROMPT, RESP, None),
            P(PROMPT, RESP, None),
            P(PROMPT, RESP, None, None),
            P(PROMPT, RESP, None, None),
            P(PROMPT, RESP, None, None),
            P(),
            P(PROMPT, RESP, None, None),
            P(PROMPT, RESP),
        ),
        out_specs=(
            P(PROMPT, RESP, None, None),
            P(PROMPT, RESP, None, None),
            P(PROMPT, RESP, None, None),
            P(PROMPT, RESP, None),
            P(PROMPT, RESP, None),
            P(),
        ),
        check_vma=False,
    )
```

```python
import functools
import math

import jax
import jax.numpy as jnp
from jax import lax
from jax.experimental import pallas as pl
from jax.experimental.pallas import tpu as pltpu
from jax.sharding import Mesh, PartitionSpec as P

HD = 128
GROUP = 5
KVH = 4
SCALE = 1.0 / math.sqrt(HD)
LOG2E = 1.4426950408889634
F32 = jnp.float32
BF16 = jnp.bfloat16

PROMPT = ("yh", "x1", "x0", "core")
RESP = ("yl", "z2", "z1", "z0")
SIZES = (4, 2, 2, 2, 2, 2, 2, 2)
Z = ("z2", "z1", "z0")


def dot(a, b, a_dim, b_dim):
    return lax.dot_general(a, b, (((a_dim,), (b_dim,)), ((), ())), preferred_element_type=F32)


def prepare_kernel(
    length_ref, q_hbm, bias_ref, do_hbm, rk_hbm, rv_hbm, qs_ref, dos_ref, rk_ref, rv_ref, q_s, do_s, arrived
):
    reads = [
        pltpu.make_async_copy(source, target, arrived.at[i])
        for i, (source, target) in enumerate(
            ((q_hbm, q_s), (do_hbm, do_s), (rk_hbm, rk_ref), (rv_hbm, rv_ref))
        )
    ]
    for read in reads:
        read.start()
    rows = q_s.shape[0]
    live = lax.broadcasted_iota(jnp.int32, (rows, HD), 0) < length_ref[0, 0]
    reads[0].wait()
    for head in range(KVH * GROUP):
        cols = slice(head * HD, (head + 1) * HD)
        span = slice(head % GROUP * rows, (head % GROUP + 1) * rows)
        bias = bias_ref[cols].reshape(1, HD)
        qs_ref[head // GROUP, span, :] = (q_s[:, cols].astype(F32) + bias).astype(BF16)
    reads[1].wait()
    for head in range(KVH * GROUP):
        cols = slice(head * HD, (head + 1) * HD)
        span = slice(head % GROUP * rows, (head % GROUP + 1) * rows)
        dos_ref[head // GROUP, span, :] = jnp.where(live, do_s[:, cols].astype(F32), 0.0).astype(BF16)
    reads[2].wait()
    reads[3].wait()


def prepared(length, queries, bias, cotangent, resp_keys, resp_values):
    rows = queries.shape[0]
    hbm = pl.BlockSpec(memory_space=pltpu.HBM)
    tall = jax.ShapeDtypeStruct((KVH, GROUP * rows, HD), BF16)
    own = jax.ShapeDtypeStruct(resp_keys.shape, BF16)
    return pl.pallas_call(
        prepare_kernel,
        out_shape=(tall, tall, own, own),
        in_specs=[
            pl.BlockSpec(memory_space=pltpu.SMEM),
            hbm,
            pl.BlockSpec(memory_space=pltpu.VMEM),
            hbm,
            hbm,
            hbm,
        ],
        scratch_shapes=[
            pltpu.VMEM(queries.shape, BF16),
            pltpu.VMEM(cotangent.shape, BF16),
            pltpu.SemaphoreType.DMA((4,)),
        ],
        compiler_params=pltpu.CompilerParams(vmem_limit_bytes=16 * 1024 * 1024),
        cost_estimate=pl.CostEstimate(
            flops=queries.size, transcendentals=0, bytes_accessed=4 * 1024 * 1024
        ),
    )(length, queries, bias, cotangent, resp_keys, resp_values)


def near_kernel(
    length_ref, qs_ref, dos_ref, rk_ref, rv_ref, near_in, expd_ref, dprobs_ref, stats_ref
):
    length = length_ref[0, 0]
    rows = rk_ref.shape[0]
    shards, both_rows, _ = near_in.shape
    shard_rows = both_rows // 2
    half = shards * shard_rows
    key_at = lax.broadcasted_iota(jnp.int32, (rows, rows), 0)
    row_at = lax.broadcasted_iota(jnp.int32, (rows, rows), 1)
    visible = (key_at <= row_at) & (key_at < length)
    for group in range(KVH):
        cols = slice(group * HD, (group + 1) * HD)
        keys, values = (
            jnp.concatenate(
                [near_in[:, at : at + shard_rows, cols].reshape(half, HD), own[:, cols]], 0
            )
            for at, own in ((0, rk_ref), (shard_rows, rv_ref))
        )
        for head in range(GROUP):
            span = slice(head * rows, (head + 1) * rows)
            scores = dot(keys, qs_ref[group, span, :], 1, 1)
            scores = jnp.concatenate(
                [scores[:half], jnp.where(visible, scores[half:], -jnp.inf)], 0
            )
            top = jnp.max(scores, 0, keepdims=True) * (SCALE * LOG2E)
            expd = jnp.exp2(scores * (SCALE * LOG2E) - top)
            dprobs = dot(values, dos_ref[group, span, :], 1, 1)
            expd_ref[group, :, span] = expd
            dprobs_ref[group, :, span] = dprobs
            stats_ref[group, 0:1, span] = top
            stats_ref[group, 1:2, span] = jnp.sum(expd, 0, keepdims=True)
            stats_ref[group, 2:3, span] = jnp.sum(expd * dprobs, 0, keepdims=True)


def near_scores(length, qs, dos, resp_keys, resp_values, near):
    shards, both_rows, _ = near.shape
    columns = qs.shape[1]
    square = (KVH, shards * both_rows // 2 + resp_keys.shape[0], columns)
    vmem = pl.BlockSpec(memory_space=pltpu.VMEM)
    return pl.pallas_call(
        near_kernel,
        out_shape=(
            jax.ShapeDtypeStruct(square, F32),
            jax.ShapeDtypeStruct(square, F32),
            jax.ShapeDtypeStruct((KVH, 8, columns), F32),
        ),
        in_specs=[pl.BlockSpec(memory_space=pltpu.SMEM), *[vmem] * 5],
        out_specs=(vmem,) * 3,
        compiler_params=pltpu.CompilerParams(vmem_limit_bytes=16 * 1024 * 1024),
        cost_estimate=pl.CostEstimate(
            flops=4 * KVH * columns * square[1] * HD,
            transcendentals=KVH * columns * square[1],
            bytes_accessed=2 * 1024 * 1024,
        ),
    )(length, qs, dos, resp_keys, resp_values, near)


def attend_kernel(
    qs_ref, dos_ref, rk_ref, near_in, far_in, expd_in, dprobs_in, stats_in,
    flat_ref, drk_ref, drv_ref, near_ref, far_ref, sums_ref, probs_s, dscores_s,
):
    rows = rk_ref.shape[0]
    shards, both_rows, _ = near_in.shape
    shard_rows = both_rows // 2
    half = shards * shard_rows
    first = half + rows
    for group in range(KVH):
        cols = slice(group * HD, (group + 1) * HD)
        far_keys = far_in[:, :shard_rows, cols].reshape(half, HD)
        far_values = far_in[:, shard_rows:, cols].reshape(half, HD)
        for head in range(GROUP):
            span = slice(head * rows, (head + 1) * rows)
            scores = dot(far_keys, qs_ref[group, span, :], 1, 1)
            near_top = stats_in[group, 0:1, span]
            top = jnp.max(scores, 0, keepdims=True) * (SCALE * LOG2E)
            top = jnp.maximum(top, near_top)
            shrink = jnp.exp2(near_top - top)
            expd = jnp.exp2(scores * (SCALE * LOG2E) - top)
            total = stats_in[group, 1:2, span] * shrink + jnp.sum(expd, 0, keepdims=True)
            inverse = 1.0 / total
            dprobs = dot(far_values, dos_ref[group, span, :], 1, 1)
            delta = stats_in[group, 2:3, span] * shrink + jnp.sum(expd * dprobs, 0, keepdims=True)
            delta = delta * inverse
            probs_s[group, first:, span] = (expd * inverse).astype(BF16)
            dscores_s[group, first:, span] = (
                expd * ((dprobs - delta) * (inverse * SCALE))
            ).astype(BF16)
            factor = shrink * inverse
            expd = expd_in[group, :, span]
            dprobs = dprobs_in[group, :, span]
            probs_s[group, :first, span] = (expd * factor).astype(BF16)
            dscores_s[group, :first, span] = (
                expd * ((dprobs - delta) * (factor * SCALE))
            ).astype(BF16)
        dscores = dscores_s[group]
        for block, left, right, own in (
            (group, dscores, qs_ref, drk_ref),
            (KVH + group, probs_s[group], dos_ref, drv_ref),
        ):
            grad = dot(left, right[group], 1, 0).astype(BF16)
            own[:, cols] = grad[half:first]
            at = slice(block * shard_rows, (block + 1) * shard_rows)
            for ref, part in ((near_ref, grad[:half]), (far_ref, grad[first:])):
                ref[:, at, :] = part.reshape(shards, shard_rows, HD)
        near_keys = near_in[:, :shard_rows, cols].reshape(half, HD)
        keys = jnp.concatenate([near_keys, rk_ref[:, cols], far_keys], 0)
        dq = dot(keys, dscores, 0, 0)
        flat_ref[group] = dq.astype(BF16)
        columns = [
            jnp.sum(dq[:, head * rows : (head + 1) * rows], 1, keepdims=True)
            for head in range(GROUP)
        ]
        columns.append(jnp.zeros((HD, HD - GROUP), F32))
        sums = jnp.concatenate(columns, 1).T[:GROUP]
        for copy in range(sums_ref.shape[0]):
            sums_ref[copy, group * GROUP : (group + 1) * GROUP, :] = sums


def attend(qs, dos, resp_keys, near, far, expd, dprobs, stats, copies):
    rows, width = resp_keys.shape
    shards, both_rows, _ = near.shape
    key_count = shards * both_rows + rows
    columns = qs.shape[1]
    vmem = pl.BlockSpec(memory_space=pltpu.VMEM)
    return pl.pallas_call(
        attend_kernel,
        out_shape=(
            jax.ShapeDtypeStruct((KVH, HD, columns), BF16),
            *[jax.ShapeDtypeStruct((rows, width), BF16)] * 2,
            *[jax.ShapeDtypeStruct((shards, both_rows * KVH, HD), BF16)] * 2,
            jax.ShapeDtypeStruct((copies, KVH * GROUP, HD), F32),
        ),
        in_specs=[vmem] * 8,
        out_specs=(vmem,) * 6,
        scratch_shapes=[pltpu.VMEM((KVH, key_count, columns), BF16)] * 2,
        compiler_params=pltpu.CompilerParams(vmem_limit_bytes=32 * 1024 * 1024),
        cost_estimate=pl.CostEstimate(
            flops=8 * KVH * columns * key_count * HD,
            transcendentals=KVH * columns * key_count // 2,
            bytes_accessed=6 * 1024 * 1024,
        ),
    )(qs, dos, resp_keys, near, far, expd, dprobs, stats)


def turn_kernel(flat_ref, out_ref):
    rows = out_ref.shape[0]
    for group in range(KVH):
        for head in range(GROUP):
            at = (group * GROUP + head) * HD
            out_ref[:, at : at + HD] = flat_ref[group, :, head * rows : (head + 1) * rows].T


def total_kernel(got, out):
    total = got[0]
    for copy in range(1, got.shape[0]):
        total = total + got[copy]
    for copy in range(out.shape[0]):
        out[copy] = total


def pair_kernel(near, got, sums, out):
    shards, data_rows, _ = near.shape
    room = (out.shape[1] - data_rows) // 2
    out[:, :data_rows, :] = (near[...].astype(F32) + got[...].astype(F32)).astype(BF16)
    total = sums[0]
    for copy in range(1, sums.shape[0]):
        total = total + sums[copy]
    total = jnp.concatenate([total, jnp.zeros((room - total.shape[0], HD), F32)], 0)
    high = total.astype(BF16).astype(F32)
    terms = jnp.concatenate([high, total - high], 0).astype(BF16)
    for shard in range(shards):
        out[shard, data_rows:, :] = terms


def finish_kernel(divisor, got, dk_ref, dv_ref, sums_ref):
    rows = dk_ref.shape[0]
    data_rows = 2 * KVH * rows
    room = (got.shape[1] - data_rows) // 2
    total = got[0].astype(F32)
    for shard in range(1, got.shape[0]):
        total = total + got[shard].astype(F32)
    for group in range(KVH):
        cols = slice(group * HD, (group + 1) * HD)
        for ref, block in ((dk_ref, group), (dv_ref, KVH + group)):
            ref[:, cols] = total[block * rows : (block + 1) * rows].astype(BF16)
    sums = total[data_rows : data_rows + room] + total[data_rows + room :]
    sums_ref[...] = sums[: sums_ref.shape[0]] / divisor


def small_call(kernel, out_shape, *operands):
    return pl.pallas_call(
        kernel,
        out_shape=out_shape,
        compiler_params=pltpu.CompilerParams(vmem_limit_bytes=8 * 1024 * 1024),
    )(*operands)


def spread(block, axis):
    copies = jnp.broadcast_to(block[None], (lax.axis_size(axis), *block.shape))
    return lax.all_to_all(copies, axis, 0, 0)


def swap(block, axis):
    return lax.ppermute(block, axis, [(0, 1), (1, 0)])


def body(
    prefix_keys, prefix_values, resp_queries, resp_keys, resp_values, query_bias, out_grad, lengths
):
    rows, width = resp_queries.shape[2:]
    shard_rows, kv_width = prefix_keys.shape[1:]
    near = spread(jnp.concatenate([prefix_keys[0], prefix_values[0]], 0), Z)
    qs, dos, rk, rv = prepared(
        lengths, resp_queries[0, 0], query_bias, out_grad[0, 0], resp_keys[0, 0], resp_values[0, 0]
    )
    first, second = ("x1", "x0", "core"), ("yh", "yl")
    far = swap(near, "yl")
    held = near_scores(lengths, qs, dos, rk, rv, near)
    flat, drk, drv, mine, others, sums = attend(
        qs, dos, rk, near, far, *held, lax.axis_size(first)
    )
    got = swap(others, "yl")
    sums = small_call(
        total_kernel,
        jax.ShapeDtypeStruct((lax.axis_size(second), *sums.shape[1:]), F32),
        lax.all_to_all(sums, first, 0, 0),
    )
    sums, flat = lax.optimization_barrier((sums, flat))
    dq = small_call(turn_kernel, jax.ShapeDtypeStruct((rows, width), BF16), flat)
    sums, dq = lax.optimization_barrier((lax.all_to_all(sums, second, 0, 0), dq))
    pairs = small_call(
        pair_kernel,
        jax.ShapeDtypeStruct((mine.shape[0], mine.shape[1] + 48, HD), BF16),
        mine, got, sums,
    )
    summed = lax.all_to_all(pairs, Z, 0, 0)
    prefix_dk, prefix_dv, sums = small_call(
        functools.partial(finish_kernel, math.sqrt(math.prod(SIZES) * rows)),
        (
            jax.ShapeDtypeStruct((shard_rows, kv_width), BF16),
            jax.ShapeDtypeStruct((shard_rows, kv_width), BF16),
            jax.ShapeDtypeStruct((KVH * GROUP, HD), F32),
        ),
        summed,
    )
    return (
        dq[None, None],
        drk[None, None],
        drv[None, None],
        prefix_dk[None],
        prefix_dv[None],
        sums.reshape(width),
    )


def solution(mesh):
    fine = Mesh(mesh.devices.reshape(SIZES), PROMPT + RESP)
    return jax.shard_map(
        body,
        mesh=fine,
        in_specs=(
            P(PROMPT, RESP, None),
            P(PROMPT, RESP, None),
            P(PROMPT, RESP, None, None),
            P(PROMPT, RESP, None, None),
            P(PROMPT, RESP, None, None),
            P(),
            P(PROMPT, RESP, None, None),
            P(PROMPT, RESP),
        ),
        out_specs=(
            P(PROMPT, RESP, None, None),
            P(PROMPT, RESP, None, None),
            P(PROMPT, RESP, None, None),
            P(PROMPT, RESP, None),
            P(PROMPT, RESP, None),
            P(),
        ),
        check_vma=False,
    )
```

```python
import functools
import math

import jax
import jax.numpy as jnp
from jax import lax
from jax.experimental import pallas as pl
from jax.experimental.pallas import tpu as pltpu
from jax.sharding import Mesh, PartitionSpec as P

HD = 128
GROUP = 5
KVH = 4
SCALE = 1.0 / math.sqrt(HD)
LOG2E = 1.4426950408889634
F32 = jnp.float32
BF16 = jnp.bfloat16

PROMPT = ("yh", "x1", "x0", "core")
RESP = ("yl", "z2", "z1", "z0")
SIZES = (4, 2, 2, 2, 2, 2, 2, 2)
Z = ("z2", "z1", "z0")


def dot(a, b, a_dim, b_dim):
    return lax.dot_general(a, b, (((a_dim,), (b_dim,)), ((), ())), preferred_element_type=F32)


def prepare_kernel(
    length_ref, q_hbm, bias_ref, do_hbm, rk_hbm, rv_hbm, qs_ref, dos_ref, rk_ref, rv_ref, q_s, do_s, arrived
):
    reads = [
        pltpu.make_async_copy(source, target, arrived.at[i])
        for i, (source, target) in enumerate(
            ((q_hbm, q_s), (do_hbm, do_s), (rk_hbm, rk_ref), (rv_hbm, rv_ref))
        )
    ]
    for read in reads:
        read.start()
    rows = q_s.shape[0]
    live = lax.broadcasted_iota(jnp.int32, (rows, HD), 0) < length_ref[0, 0]
    reads[0].wait()
    for head in range(KVH * GROUP):
        cols = slice(head * HD, (head + 1) * HD)
        span = slice(head % GROUP * rows, (head % GROUP + 1) * rows)
        bias = bias_ref[cols].reshape(1, HD)
        qs_ref[head // GROUP, span, :] = (q_s[:, cols].astype(F32) + bias).astype(BF16)
    reads[1].wait()
    for head in range(KVH * GROUP):
        cols = slice(head * HD, (head + 1) * HD)
        span = slice(head % GROUP * rows, (head % GROUP + 1) * rows)
        dos_ref[head // GROUP, span, :] = jnp.where(live, do_s[:, cols].astype(F32), 0.0).astype(BF16)
    reads[2].wait()
    reads[3].wait()


def prepared(length, queries, bias, cotangent, resp_keys, resp_values):
    rows = queries.shape[0]
    hbm = pl.BlockSpec(memory_space=pltpu.HBM)
    tall = jax.ShapeDtypeStruct((KVH, GROUP * rows, HD), BF16)
    own = jax.ShapeDtypeStruct(resp_keys.shape, BF16)
    return pl.pallas_call(
        prepare_kernel,
        out_shape=(tall, tall, own, own),
        in_specs=[
            pl.BlockSpec(memory_space=pltpu.SMEM),
            hbm,
            pl.BlockSpec(memory_space=pltpu.VMEM),
            hbm,
            hbm,
            hbm,
        ],
        scratch_shapes=[
            pltpu.VMEM(queries.shape, BF16),
            pltpu.VMEM(cotangent.shape, BF16),
            pltpu.SemaphoreType.DMA((4,)),
        ],
        compiler_params=pltpu.CompilerParams(vmem_limit_bytes=16 * 1024 * 1024),
        cost_estimate=pl.CostEstimate(
            flops=queries.size, transcendentals=0, bytes_accessed=4 * 1024 * 1024
        ),
    )(length, queries, bias, cotangent, resp_keys, resp_values)


def near_kernel(
    length_ref, qs_ref, dos_ref, rk_ref, rv_ref, near_in, expd_ref, dprobs_ref, stats_ref
):
    length = length_ref[0, 0]
    rows = rk_ref.shape[0]
    shards, both_rows, _ = near_in.shape
    shard_rows = both_rows // 2
    half = shards * shard_rows
    key_at = lax.broadcasted_iota(jnp.int32, (rows, rows), 0)
    row_at = lax.broadcasted_iota(jnp.int32, (rows, rows), 1)
    visible = (key_at <= row_at) & (key_at < length)
    for group in range(KVH):
        cols = slice(group * HD, (group + 1) * HD)
        keys, values = (
            jnp.concatenate(
                [near_in[:, at : at + shard_rows, cols].reshape(half, HD), own[:, cols]], 0
            )
            for at, own in ((0, rk_ref), (shard_rows, rv_ref))
        )
        for head in range(GROUP):
            span = slice(head * rows, (head + 1) * rows)
            scores = dot(keys, qs_ref[group, span, :], 1, 1)
            scores = jnp.concatenate(
                [scores[:half], jnp.where(visible, scores[half:], -jnp.inf)], 0
            )
            top = jnp.max(scores, 0, keepdims=True) * (SCALE * LOG2E)
            expd = jnp.exp2(scores * (SCALE * LOG2E) - top)
            dprobs = dot(values, dos_ref[group, span, :], 1, 1)
            expd_ref[group, :, span] = expd
            dprobs_ref[group, :, span] = dprobs
            stats_ref[group, 0:1, span] = top
            stats_ref[group, 1:2, span] = jnp.sum(expd, 0, keepdims=True)
            stats_ref[group, 2:3, span] = jnp.sum(expd * dprobs, 0, keepdims=True)


def near_scores(length, qs, dos, resp_keys, resp_values, near):
    shards, both_rows, _ = near.shape
    columns = qs.shape[1]
    square = (KVH, shards * both_rows // 2 + resp_keys.shape[0], columns)
    vmem = pl.BlockSpec(memory_space=pltpu.VMEM)
    return pl.pallas_call(
        near_kernel,
        out_shape=(
            jax.ShapeDtypeStruct(square, F32),
            jax.ShapeDtypeStruct(square, F32),
            jax.ShapeDtypeStruct((KVH, 8, columns), F32),
        ),
        in_specs=[pl.BlockSpec(memory_space=pltpu.SMEM), *[vmem] * 5],
        out_specs=(vmem,) * 3,
        compiler_params=pltpu.CompilerParams(vmem_limit_bytes=16 * 1024 * 1024),
        cost_estimate=pl.CostEstimate(
            flops=4 * KVH * columns * square[1] * HD,
            transcendentals=KVH * columns * square[1],
            bytes_accessed=2 * 1024 * 1024,
        ),
    )(length, qs, dos, resp_keys, resp_values, near)


def attend_kernel(
    qs_ref, dos_ref, rk_ref, near_in, far_in, expd_in, dprobs_in, stats_in,
    flat_ref, drk_ref, drv_ref, near_ref, far_ref, sums_ref, probs_s, dscores_s,
):
    rows = rk_ref.shape[0]
    shards, both_rows, _ = near_in.shape
    shard_rows = both_rows // 2
    half = shards * shard_rows
    first = half + rows
    for group in range(KVH):
        cols = slice(group * HD, (group + 1) * HD)
        far_keys = far_in[:, :shard_rows, cols].reshape(half, HD)
        far_values = far_in[:, shard_rows:, cols].reshape(half, HD)
        for head in range(GROUP):
            span = slice(head * rows, (head + 1) * rows)
            scores = dot(far_keys, qs_ref[group, span, :], 1, 1)
            near_top = stats_in[group, 0:1, span]
            top = jnp.max(scores, 0, keepdims=True) * (SCALE * LOG2E)
            top = jnp.maximum(top, near_top)
            shrink = jnp.exp2(near_top - top)
            expd = jnp.exp2(scores * (SCALE * LOG2E) - top)
            total = stats_in[group, 1:2, span] * shrink + jnp.sum(expd, 0, keepdims=True)
            inverse = 1.0 / total
            dprobs = dot(far_values, dos_ref[group, span, :], 1, 1)
            delta = stats_in[group, 2:3, span] * shrink + jnp.sum(expd * dprobs, 0, keepdims=True)
            delta = delta * inverse
            probs_s[group, first:, span] = (expd * inverse).astype(BF16)
            dscores_s[group, first:, span] = (
                expd * ((dprobs - delta) * (inverse * SCALE))
            ).astype(BF16)
            factor = shrink * inverse
            expd = expd_in[group, :, span]
            dprobs = dprobs_in[group, :, span]
            probs_s[group, :first, span] = (expd * factor).astype(BF16)
            dscores_s[group, :first, span] = (
                expd * ((dprobs - delta) * (factor * SCALE))
            ).astype(BF16)
    for group in range(KVH):
        cols = slice(group * HD, (group + 1) * HD)
        dscores = dscores_s[group]
        for block, left, right, own in (
            (group, dscores, qs_ref, drk_ref),
            (KVH + group, probs_s[group], dos_ref, drv_ref),
        ):
            grad = dot(left, right[group], 1, 0).astype(BF16)
            own[:, cols] = grad[half:first]
            at = slice(block * shard_rows, (block + 1) * shard_rows)
            for ref, part in ((near_ref, grad[:half]), (far_ref, grad[first:])):
                ref[:, at, :] = part.reshape(shards, shard_rows, HD)
        near_keys, far_keys = (ref[:, :shard_rows, cols].reshape(half, HD) for ref in (near_in, far_in))
        keys = jnp.concatenate([near_keys, rk_ref[:, cols], far_keys], 0)
        dq = dot(keys, dscores, 0, 0)
        flat_ref[group] = dq.astype(BF16)
        columns = [
            jnp.sum(dq[:, head * rows : (head + 1) * rows], 1, keepdims=True)
            for head in range(GROUP)
        ]
        columns.append(jnp.zeros((HD, HD - GROUP), F32))
        sums = jnp.concatenate(columns, 1).T[:GROUP]
        for copy in range(sums_ref.shape[0]):
            sums_ref[copy, group * GROUP : (group + 1) * GROUP, :] = sums


def attend(qs, dos, resp_keys, near, far, expd, dprobs, stats, copies):
    rows, width = resp_keys.shape
    shards, both_rows, _ = near.shape
    key_count = shards * both_rows + rows
    columns = qs.shape[1]
    vmem = pl.BlockSpec(memory_space=pltpu.VMEM)
    return pl.pallas_call(
        attend_kernel,
        out_shape=(
            jax.ShapeDtypeStruct((KVH, HD, columns), BF16),
            *[jax.ShapeDtypeStruct((rows, width), BF16)] * 2,
            *[jax.ShapeDtypeStruct((shards, both_rows * KVH, HD), BF16)] * 2,
            jax.ShapeDtypeStruct((copies, KVH * GROUP, HD), F32),
        ),
        in_specs=[vmem] * 8,
        out_specs=(vmem,) * 6,
        scratch_shapes=[pltpu.VMEM((KVH, key_count, columns), BF16)] * 2,
        compiler_params=pltpu.CompilerParams(vmem_limit_bytes=32 * 1024 * 1024),
        cost_estimate=pl.CostEstimate(
            flops=8 * KVH * columns * key_count * HD,
            transcendentals=KVH * columns * key_count // 2,
            bytes_accessed=6 * 1024 * 1024,
        ),
    )(qs, dos, resp_keys, near, far, expd, dprobs, stats)


def turn_kernel(flat_ref, out_ref):
    rows = out_ref.shape[0]
    for group in range(KVH):
        for head in range(GROUP):
            at = (group * GROUP + head) * HD
            out_ref[:, at : at + HD] = flat_ref[group, :, head * rows : (head + 1) * rows].T


def total_kernel(got, out):
    total = got[0]
    for copy in range(1, got.shape[0]):
        total = total + got[copy]
    for copy in range(out.shape[0]):
        out[copy] = total


def pair_kernel(near, got, sums, out):
    shards, data_rows, _ = near.shape
    room = (out.shape[1] - data_rows) // 2
    out[:, :data_rows, :] = (near[...].astype(F32) + got[...].astype(F32)).astype(BF16)
    total = sums[0]
    for copy in range(1, sums.shape[0]):
        total = total + sums[copy]
    total = jnp.concatenate([total, jnp.zeros((room - total.shape[0], HD), F32)], 0)
    high = total.astype(BF16).astype(F32)
    terms = jnp.concatenate([high, total - high], 0).astype(BF16)
    for shard in range(shards):
        out[shard, data_rows:, :] = terms


def finish_kernel(divisor, got, dk_ref, dv_ref, sums_ref):
    rows = dk_ref.shape[0]
    data_rows = 2 * KVH * rows
    room = (got.shape[1] - data_rows) // 2
    total = got[0].astype(F32)
    for shard in range(1, got.shape[0]):
        total = total + got[shard].astype(F32)
    for group in range(KVH):
        cols = slice(group * HD, (group + 1) * HD)
        for ref, block in ((dk_ref, group), (dv_ref, KVH + group)):
            ref[:, cols] = total[block * rows : (block + 1) * rows].astype(BF16)
    sums = total[data_rows : data_rows + room] + total[data_rows + room :]
    sums_ref[...] = sums[: sums_ref.shape[0]] / divisor


def small_call(kernel, out_shape, *operands):
    return pl.pallas_call(
        kernel,
        out_shape=out_shape,
        compiler_params=pltpu.CompilerParams(vmem_limit_bytes=8 * 1024 * 1024),
    )(*operands)


def spread(block, axis):
    copies = jnp.broadcast_to(block[None], (lax.axis_size(axis), *block.shape))
    return lax.all_to_all(copies, axis, 0, 0)


def swap(block, axis):
    return lax.ppermute(block, axis, [(0, 1), (1, 0)])


def body(
    prefix_keys, prefix_values, resp_queries, resp_keys, resp_values, query_bias, out_grad, lengths
):
    rows, width = resp_queries.shape[2:]
    shard_rows, kv_width = prefix_keys.shape[1:]
    near = spread(jnp.concatenate([prefix_keys[0], prefix_values[0]], 0), Z)
    qs, dos, rk, rv = prepared(
        lengths, resp_queries[0, 0], query_bias, out_grad[0, 0], resp_keys[0, 0], resp_values[0, 0]
    )
    first, second = ("x1", "x0", "core"), ("yh", "yl")
    far = swap(near, "yl")
    held = near_scores(lengths, qs, dos, rk, rv, near)
    flat, drk, drv, mine, others, sums = attend(
        qs, dos, rk, near, far, *held, lax.axis_size(first)
    )
    got = swap(others, "yl")
    sums = small_call(
        total_kernel,
        jax.ShapeDtypeStruct((lax.axis_size(second), *sums.shape[1:]), F32),
        lax.all_to_all(sums, first, 0, 0),
    )
    sums, flat = lax.optimization_barrier((sums, flat))
    dq = small_call(turn_kernel, jax.ShapeDtypeStruct((rows, width), BF16), flat)
    sums, dq = lax.optimization_barrier((lax.all_to_all(sums, second, 0, 0), dq))
    pairs = small_call(
        pair_kernel,
        jax.ShapeDtypeStruct((mine.shape[0], mine.shape[1] + 48, HD), BF16),
        mine, got, sums,
    )
    summed = lax.all_to_all(pairs, Z, 0, 0)
    prefix_dk, prefix_dv, sums = small_call(
        functools.partial(finish_kernel, math.sqrt(math.prod(SIZES) * rows)),
        (
            jax.ShapeDtypeStruct((shard_rows, kv_width), BF16),
            jax.ShapeDtypeStruct((shard_rows, kv_width), BF16),
            jax.ShapeDtypeStruct((KVH * GROUP, HD), F32),
        ),
        summed,
    )
    return (
        dq[None, None],
        drk[None, None],
        drv[None, None],
        prefix_dk[None],
        prefix_dv[None],
        sums.reshape(width),
    )


def solution(mesh):
    fine = Mesh(mesh.devices.reshape(SIZES), PROMPT + RESP)
    return jax.shard_map(
        body,
        mesh=fine,
        in_specs=(
            P(PROMPT, RESP, None),
            P(PROMPT, RESP, None),
            P(PROMPT, RESP, None, None),
            P(PROMPT, RESP, None, None),
            P(PROMPT, RESP, None, None),
            P(),
            P(PROMPT, RESP, None, None),
            P(PROMPT, RESP),
        ),
        out_specs=(
            P(PROMPT, RESP, None, None),
            P(PROMPT, RESP, None, None),
            P(PROMPT, RESP, None, None),
            P(PROMPT, RESP, None),
            P(PROMPT, RESP, None),
            P(),
        ),
        check_vma=False,
    )
```

```python
import functools
import math

import jax
import jax.numpy as jnp
from jax import lax
from jax.experimental import pallas as pl
from jax.experimental.pallas import tpu as pltpu
from jax.sharding import Mesh, PartitionSpec as P

HD = 128
GROUP = 5
KVH = 4
SCALE = 1.0 / math.sqrt(HD)
LOG2E = 1.4426950408889634
F32 = jnp.float32
BF16 = jnp.bfloat16

PROMPT = ("yh", "x1", "x0", "core")
RESP = ("yl", "z2", "z1", "z0")
SIZES = (4, 2, 2, 2, 2, 2, 2, 2)
Z = ("z1", "z0", "z2")


def dot(a, b, a_dim, b_dim):
    return lax.dot_general(a, b, (((a_dim,), (b_dim,)), ((), ())), preferred_element_type=F32)


def prepare_kernel(
    length_ref, q_hbm, bias_ref, do_hbm, rk_hbm, rv_hbm, qs_ref, dos_ref, rk_ref, rv_ref, q_s, do_s, arrived
):
    reads = [
        pltpu.make_async_copy(source, target, arrived.at[i])
        for i, (source, target) in enumerate(
            ((q_hbm, q_s), (do_hbm, do_s), (rk_hbm, rk_ref), (rv_hbm, rv_ref))
        )
    ]
    for read in reads:
        read.start()
    rows = q_s.shape[0]
    live = lax.broadcasted_iota(jnp.int32, (rows, HD), 0) < length_ref[0, 0]
    reads[0].wait()
    for head in range(KVH * GROUP):
        cols = slice(head * HD, (head + 1) * HD)
        span = slice(head % GROUP * rows, (head % GROUP + 1) * rows)
        bias = bias_ref[cols].reshape(1, HD)
        qs_ref[head // GROUP, span, :] = (q_s[:, cols].astype(F32) + bias).astype(BF16)
    reads[1].wait()
    for head in range(KVH * GROUP):
        cols = slice(head * HD, (head + 1) * HD)
        span = slice(head % GROUP * rows, (head % GROUP + 1) * rows)
        dos_ref[head // GROUP, span, :] = jnp.where(live, do_s[:, cols].astype(F32), 0.0).astype(BF16)
    reads[2].wait()
    reads[3].wait()


def prepared(length, queries, bias, cotangent, resp_keys, resp_values):
    rows = queries.shape[0]
    hbm = pl.BlockSpec(memory_space=pltpu.HBM)
    tall = jax.ShapeDtypeStruct((KVH, GROUP * rows, HD), BF16)
    own = jax.ShapeDtypeStruct(resp_keys.shape, BF16)
    return pl.pallas_call(
        prepare_kernel,
        out_shape=(tall, tall, own, own),
        in_specs=[
            pl.BlockSpec(memory_space=pltpu.SMEM),
            hbm,
            pl.BlockSpec(memory_space=pltpu.VMEM),
            hbm,
            hbm,
            hbm,
        ],
        scratch_shapes=[
            pltpu.VMEM(queries.shape, BF16),
            pltpu.VMEM(cotangent.shape, BF16),
            pltpu.SemaphoreType.DMA((4,)),
        ],
        compiler_params=pltpu.CompilerParams(vmem_limit_bytes=16 * 1024 * 1024),
        cost_estimate=pl.CostEstimate(
            flops=queries.size, transcendentals=0, bytes_accessed=4 * 1024 * 1024
        ),
    )(length, queries, bias, cotangent, resp_keys, resp_values)


def near_kernel(
    length_ref, qs_ref, dos_ref, rk_ref, rv_ref, near_in, expd_ref, dprobs_ref, stats_ref
):
    length = length_ref[0, 0]
    rows = rk_ref.shape[0]
    shards, both_rows, _ = near_in.shape
    shard_rows = both_rows // 2
    half = shards * shard_rows
    key_at = lax.broadcasted_iota(jnp.int32, (rows, rows), 0)
    row_at = lax.broadcasted_iota(jnp.int32, (rows, rows), 1)
    visible = (key_at <= row_at) & (key_at < length)
    for group in range(KVH):
        cols = slice(group * HD, (group + 1) * HD)
        keys, values = (
            jnp.concatenate(
                [near_in[:, at : at + shard_rows, cols].reshape(half, HD), own[:, cols]], 0
            )
            for at, own in ((0, rk_ref), (shard_rows, rv_ref))
        )
        for head in range(GROUP):
            span = slice(head * rows, (head + 1) * rows)
            scores = dot(keys, qs_ref[group, span, :], 1, 1)
            scores = jnp.concatenate(
                [scores[:half], jnp.where(visible, scores[half:], -jnp.inf)], 0
            )
            top = jnp.max(scores, 0, keepdims=True) * (SCALE * LOG2E)
            expd = jnp.exp2(scores * (SCALE * LOG2E) - top)
            dprobs = dot(values, dos_ref[group, span, :], 1, 1)
            expd_ref[group, :, span] = expd
            dprobs_ref[group, :, span] = dprobs
            stats_ref[group, 0:1, span] = top
            stats_ref[group, 1:2, span] = jnp.sum(expd, 0, keepdims=True)
            stats_ref[group, 2:3, span] = jnp.sum(expd * dprobs, 0, keepdims=True)


def near_scores(length, qs, dos, resp_keys, resp_values, near):
    shards, both_rows, _ = near.shape
    columns = qs.shape[1]
    square = (KVH, shards * both_rows // 2 + resp_keys.shape[0], columns)
    vmem = pl.BlockSpec(memory_space=pltpu.VMEM)
    return pl.pallas_call(
        near_kernel,
        out_shape=(
            jax.ShapeDtypeStruct(square, F32),
            jax.ShapeDtypeStruct(square, F32),
            jax.ShapeDtypeStruct((KVH, 8, columns), F32),
        ),
        in_specs=[pl.BlockSpec(memory_space=pltpu.SMEM), *[vmem] * 5],
        out_specs=(vmem,) * 3,
        compiler_params=pltpu.CompilerParams(vmem_limit_bytes=16 * 1024 * 1024),
        cost_estimate=pl.CostEstimate(
            flops=4 * KVH * columns * square[1] * HD,
            transcendentals=KVH * columns * square[1],
            bytes_accessed=2 * 1024 * 1024,
        ),
    )(length, qs, dos, resp_keys, resp_values, near)


def attend_kernel(
    qs_ref, dos_ref, rk_ref, near_in, far_in, expd_in, dprobs_in, stats_in,
    flat_ref, drk_ref, drv_ref, near_ref, far_ref, sums_ref, probs_s, dscores_s,
):
    rows = rk_ref.shape[0]
    shards, both_rows, _ = near_in.shape
    shard_rows = both_rows // 2
    half = shards * shard_rows
    first = half + rows
    for group in range(KVH):
        cols = slice(group * HD, (group + 1) * HD)
        far_keys = far_in[:, :shard_rows, cols].reshape(half, HD)
        far_values = far_in[:, shard_rows:, cols].reshape(half, HD)
        for head in range(GROUP):
            span = slice(head * rows, (head + 1) * rows)
            scores = dot(far_keys, qs_ref[group, span, :], 1, 1)
            near_top = stats_in[group, 0:1, span]
            top = jnp.max(scores, 0, keepdims=True) * (SCALE * LOG2E)
            top = jnp.maximum(top, near_top)
            shrink = jnp.exp2(near_top - top)
            expd = jnp.exp2(scores * (SCALE * LOG2E) - top)
            total = stats_in[group, 1:2, span] * shrink + jnp.sum(expd, 0, keepdims=True)
            inverse = 1.0 / total
            dprobs = dot(far_values, dos_ref[group, span, :], 1, 1)
            delta = stats_in[group, 2:3, span] * shrink + jnp.sum(expd * dprobs, 0, keepdims=True)
            delta = delta * inverse
            probs_s[group, first:, span] = (expd * inverse).astype(BF16)
            dscores_s[group, first:, span] = (
                expd * ((dprobs - delta) * (inverse * SCALE))
            ).astype(BF16)
            factor = shrink * inverse
            expd = expd_in[group, :, span]
            dprobs = dprobs_in[group, :, span]
            probs_s[group, :first, span] = (expd * factor).astype(BF16)
            dscores_s[group, :first, span] = (
                expd * ((dprobs - delta) * (factor * SCALE))
            ).astype(BF16)
    for group in range(KVH):
        cols = slice(group * HD, (group + 1) * HD)
        dscores = dscores_s[group]
        for block, left, right, own in (
            (group, dscores, qs_ref, drk_ref),
            (KVH + group, probs_s[group], dos_ref, drv_ref),
        ):
            grad = dot(left, right[group], 1, 0).astype(BF16)
            own[:, cols] = grad[half:first]
            at = slice(block * shard_rows, (block + 1) * shard_rows)
            for ref, part in ((near_ref, grad[:half]), (far_ref, grad[first:])):
                ref[:, at, :] = part.reshape(shards, shard_rows, HD)
        near_keys, far_keys = (ref[:, :shard_rows, cols].reshape(half, HD) for ref in (near_in, far_in))
        keys = jnp.concatenate([near_keys, rk_ref[:, cols], far_keys], 0)
        dq = dot(keys, dscores, 0, 0)
        flat_ref[group] = dq.astype(BF16)
        columns = [
            jnp.sum(dq[:, head * rows : (head + 1) * rows], 1, keepdims=True)
            for head in range(GROUP)
        ]
        columns.append(jnp.zeros((HD, HD - GROUP), F32))
        sums = jnp.concatenate(columns, 1).T[:GROUP]
        for copy in range(sums_ref.shape[0]):
            sums_ref[copy, group * GROUP : (group + 1) * GROUP, :] = sums


def attend(qs, dos, resp_keys, near, far, expd, dprobs, stats, copies):
    rows, width = resp_keys.shape
    shards, both_rows, _ = near.shape
    key_count = shards * both_rows + rows
    columns = qs.shape[1]
    vmem = pl.BlockSpec(memory_space=pltpu.VMEM)
    return pl.pallas_call(
        attend_kernel,
        out_shape=(
            jax.ShapeDtypeStruct((KVH, HD, columns), BF16),
            *[jax.ShapeDtypeStruct((rows, width), BF16)] * 2,
            *[jax.ShapeDtypeStruct((shards, both_rows * KVH, HD), BF16)] * 2,
            jax.ShapeDtypeStruct((copies, KVH * GROUP, HD), F32),
        ),
        in_specs=[vmem] * 8,
        out_specs=(vmem,) * 6,
        scratch_shapes=[pltpu.VMEM((KVH, key_count, columns), BF16)] * 2,
        compiler_params=pltpu.CompilerParams(vmem_limit_bytes=32 * 1024 * 1024),
        cost_estimate=pl.CostEstimate(
            flops=8 * KVH * columns * key_count * HD,
            transcendentals=KVH * columns * key_count // 2,
            bytes_accessed=6 * 1024 * 1024,
        ),
    )(qs, dos, resp_keys, near, far, expd, dprobs, stats)


def turn_kernel(flat_ref, out_ref):
    rows = out_ref.shape[0]
    for group in range(KVH):
        for head in range(GROUP):
            at = (group * GROUP + head) * HD
            out_ref[:, at : at + HD] = flat_ref[group, :, head * rows : (head + 1) * rows].T


def total_kernel(got, out):
    total = got[0]
    for copy in range(1, got.shape[0]):
        total = total + got[copy]
    for copy in range(out.shape[0]):
        out[copy] = total


def pair_kernel(near, got, sums, out):
    shards, data_rows, _ = near.shape
    room = (out.shape[1] - data_rows) // 2
    out[:, :data_rows, :] = (near[...].astype(F32) + got[...].astype(F32)).astype(BF16)
    total = sums[0]
    for copy in range(1, sums.shape[0]):
        total = total + sums[copy]
    total = jnp.concatenate([total, jnp.zeros((room - total.shape[0], HD), F32)], 0)
    high = total.astype(BF16).astype(F32)
    terms = jnp.concatenate([high, total - high], 0).astype(BF16)
    for shard in range(shards):
        out[shard, data_rows:, :] = terms


def finish_kernel(divisor, got, dk_ref, dv_ref, sums_ref):
    rows = dk_ref.shape[0]
    data_rows = 2 * KVH * rows
    room = (got.shape[1] - data_rows) // 2
    total = got[0].astype(F32)
    for shard in range(1, got.shape[0]):
        total = total + got[shard].astype(F32)
    for group in range(KVH):
        cols = slice(group * HD, (group + 1) * HD)
        for ref, block in ((dk_ref, group), (dv_ref, KVH + group)):
            ref[:, cols] = total[block * rows : (block + 1) * rows].astype(BF16)
    sums = total[data_rows : data_rows + room] + total[data_rows + room :]
    sums_ref[...] = sums[: sums_ref.shape[0]] / divisor


def small_call(kernel, out_shape, *operands):
    return pl.pallas_call(
        kernel,
        out_shape=out_shape,
        compiler_params=pltpu.CompilerParams(vmem_limit_bytes=8 * 1024 * 1024),
    )(*operands)


def spread(block, axis):
    copies = jnp.broadcast_to(block[None], (lax.axis_size(axis), *block.shape))
    return lax.all_to_all(copies, axis, 0, 0)


def swap(block, axis):
    return lax.ppermute(block, axis, [(0, 1), (1, 0)])


def body(
    prefix_keys, prefix_values, resp_queries, resp_keys, resp_values, query_bias, out_grad, lengths
):
    rows, width = resp_queries.shape[2:]
    shard_rows, kv_width = prefix_keys.shape[1:]
    near = spread(jnp.concatenate([prefix_keys[0], prefix_values[0]], 0), Z)
    qs, dos, rk, rv = prepared(
        lengths, resp_queries[0, 0], query_bias, out_grad[0, 0], resp_keys[0, 0], resp_values[0, 0]
    )
    first, second = ("x1", "x0", "core"), ("yh", "yl")
    far = swap(near, "yl")
    held = near_scores(lengths, qs, dos, rk, rv, near)
    flat, drk, drv, mine, others, sums = attend(
        qs, dos, rk, near, far, *held, lax.axis_size(first)
    )
    got = swap(others, "yl")
    sums = small_call(
        total_kernel,
        jax.ShapeDtypeStruct((lax.axis_size(second), *sums.shape[1:]), F32),
        lax.all_to_all(sums, first, 0, 0),
    )
    sums, flat = lax.optimization_barrier((sums, flat))
    dq = small_call(turn_kernel, jax.ShapeDtypeStruct((rows, width), BF16), flat)
    sums, dq = lax.optimization_barrier((lax.all_to_all(sums, second, 0, 0), dq))
    pairs = small_call(
        pair_kernel,
        jax.ShapeDtypeStruct((mine.shape[0], mine.shape[1] + 48, HD), BF16),
        mine, got, sums,
    )
    summed = lax.all_to_all(pairs, Z, 0, 0)
    prefix_dk, prefix_dv, sums = small_call(
        functools.partial(finish_kernel, math.sqrt(math.prod(SIZES) * rows)),
        (
            jax.ShapeDtypeStruct((shard_rows, kv_width), BF16),
            jax.ShapeDtypeStruct((shard_rows, kv_width), BF16),
            jax.ShapeDtypeStruct((KVH * GROUP, HD), F32),
        ),
        summed,
    )
    return (
        dq[None, None],
        drk[None, None],
        drv[None, None],
        prefix_dk[None],
        prefix_dv[None],
        sums.reshape(width),
    )


def solution(mesh):
    fine = Mesh(mesh.devices.reshape(SIZES), PROMPT + RESP)
    return jax.shard_map(
        body,
        mesh=fine,
        in_specs=(
            P(PROMPT, RESP, None),
            P(PROMPT, RESP, None),
            P(PROMPT, RESP, None, None),
            P(PROMPT, RESP, None, None),
            P(PROMPT, RESP, None, None),
            P(),
            P(PROMPT, RESP, None, None),
            P(PROMPT, RESP),
        ),
        out_specs=(
            P(PROMPT, RESP, None, None),
            P(PROMPT, RESP, None, None),
            P(PROMPT, RESP, None, None),
            P(PROMPT, RESP, None),
            P(PROMPT, RESP, None),
            P(),
        ),
        check_vma=False,
    )
```
